1024 devices in a mesh: pipe: 8 (over y_hi, core), expert: 64 (over z, x), dp: 2 (over y_lo).
Axes of the slice: x: 8, y: 8 (y_hi: 4, y_lo: 2; y = y_hi * 2 + y_lo), z: 8, core: 2. Of those that a mesh axis runs over, the one named last changes fastest.
Arguments:
- tokens: bfloat16 [2048, 4096], P(('expert', 'dp'), 'pipe'), may hold values from -6 to 6
- cotangent: bfloat16 [2048, 4096], P(('expert', 'dp'), 'pipe'), may hold values from -1.5 to 1.5
- routes: int32 [2048, 8], P(('expert', 'dp')), may hold values from 0 to 63, all different within a row; in each aligned block of 16 rows (0 to 15, 16 to 31, ...) at most 3 rows name the same one
- gates: float32 [2048, 8], P(('expert', 'dp')), may hold values from 0.1 to 1
- w_gate: bfloat16 [64, 4096, 1024], P('expert', 'pipe'), may hold values from -0.09375 to 0.09375
- w_up: bfloat16 [64, 4096, 1024], P('expert', 'pipe'), may hold values from -0.09375 to 0.09375
- w_down: bfloat16 [64, 1024, 4096], P('expert', None, 'pipe'), may hold values from -0.1875 to 0.1875
Outputs:
- mixed: bfloat16 [2048, 4096], P(('expert', 'dp'), 'pipe')
- token_grad: bfloat16 [2048, 4096], P(('expert', 'dp'), 'pipe')
- grad_gate: bfloat16 [64, 4096, 1024], P('expert', 'pipe', 'dp')
- grad_up: bfloat16 [64, 4096, 1024], P('expert', 'pipe', 'dp')
- grad_down: bfloat16 [64, 1024, 4096], P('expert', 'dp', 'pipe')
The draws below stay inside these ranges and needn't reach their ends.
Inputs may be any that keep to these rules, and one draw needn't show every extreme that they name: `routes`: each token names 8 different experts. Within the 16 rows of one device no expert is named more than 3 times, a bound that some block reaches.
All inputs are finite; a program needn't handle non-finite values.
Results may differ from the reference program's by a relative error of at most 0.0065.
Values may be sent and summed in bfloat16 or wider, within the bound.
A program may use at most 32 MiB of HBM per device.

```python
import math
import jax
import jax.numpy as jnp
import numpy as np
from jax import lax

D = 4096
FF = 1024
TOK_DEV = 16
EXPERTS = 64
TOP = 8
CAP = 3
TOKENS = 2048
N_EXPERT = 64
N_DP = 2


def steps_of(own_key, dims, cuts, smallest, largest):
    level, own = 1.0, jax.random.fold_in(own_key, 6)
    for dim, shards_of in cuts:
        steps = jnp.exp(jax.random.uniform(jax.random.fold_in(own, dim), (shards_of,), jnp.float32, smallest / len(cuts), largest / len(cuts)))
        level = level * jnp.repeat(steps, dims[dim] // shards_of).reshape([-1 if axis == dim else 1 for axis in range(len(dims))])
    return level


def shared_out(own_key, own, number, rows, amount, top, limit, skew):
    order = jax.random.permutation(own_key, amount)
    heavy_load, ordinary = load_shares(amount, rows * top, limit, skew, True), load_shares(amount, rows * top, limit, skew, False)
    places = jnp.arange(amount)

    def named(lengths, rotation):
        used = int((lengths > 0).sum())
        fixed = max(1, used // 4)
        moved = fixed + (places - fixed + rotation * (used - fixed)) % max(1, amount - fixed)
        return jnp.zeros((amount,), jnp.int32).at[order[jnp.where(places < fixed, places, moved)]].set(jnp.asarray(lengths, jnp.int32))

    lengths = jnp.where(number % 4 == 0, named(heavy_load, number // 4), named(ordinary, number - number // 4 - 1))
    mixed = jax.random.permutation(jax.random.fold_in(own, 3), amount)
    donor, taker = mixed[0:amount // 2 * 2:2], mixed[1:amount // 2 * 2:2]
    margin = jnp.minimum(lengths[donor] - 1, limit - lengths[taker]) // 2
    margin = jnp.where((donor == order[0]) | (taker == order[0]) | (lengths[taker] == 0), 0, jnp.maximum(margin, 0))
    moved = jax.random.randint(jax.random.fold_in(own, 4), (amount // 2,), 0, 1 << 20) % (margin + 1)
    lengths = lengths.at[donor].add(-moved).at[taker].add(moved)
    items = jnp.searchsorted(jnp.cumsum(lengths), jnp.arange(rows * top), side="right").astype(jnp.int32)
    grid = items.reshape(top, rows).T
    grid = grid[jax.random.permutation(jax.random.fold_in(own, 1), rows)]
    rotation = jax.random.randint(jax.random.fold_in(own, 2), (rows, 1), 0, top)
    return jnp.take_along_axis(grid, (jnp.arange(top)[None, :] + rotation) % top, axis=1)


def load_shares(count, total, bound, lean, full):
    weights = [(1 << 20) // math.isqrt(standing ** lean) + 1 for standing in range(1, count + 1)]
    largest = bound if full else min(bound, max(-(-total // count), total * weights[0] // sum(weights)))
    least = 1 if total - largest >= count - 1 else 0
    given, spare = [largest] + [least] * (count - 1), total - largest - least * (count - 1)
    while spare > 0:
        candidates = [i for i in range(1, count) if given[i] < largest] or [i for i in range(1, count) if given[i] < bound]
        whole, remaining = sum([weights[i] for i in candidates]), spare
        for i in candidates:
            extra = min(bound - given[i], max(1, remaining * weights[i] // whole), spare)
            given[i] = given[i] + extra
            spare = spare - extra
    return np.array(given)


def normal_values(rng, shape, deviation, reach, pieces=(), held_as=jnp.bfloat16):
    result = deviation * jax.random.normal(rng, shape, jnp.float32)
    if pieces:
        result = result * steps_of(rng, shape, pieces, -0.22, 0.18)
    return jnp.clip(result, -reach, reach).astype(held_as)


def setup_inputs(seed: int = 0) -> dict:
    keys = jax.random.split(jax.random.key(seed), 8)
    tokens = normal_values(keys[0], (TOKENS, D), 1.0, 6.0, ((0, 128), (1, 8)))
    cotangent = normal_values(keys[1], (TOKENS, D), 0.25, 1.5, ((0, 128), (1, 8)))
    routes_keys = jax.random.split(jax.random.fold_in(keys[2], 1), TOKENS // TOK_DEV)
    routes_turns = jax.random.permutation(jax.random.fold_in(keys[2], 3), TOKENS // TOK_DEV)
    routes = jax.vmap(lambda own, number: shared_out(jax.random.fold_in(keys[2], 2), own, number, TOK_DEV, EXPERTS, TOP, CAP, 2))(routes_keys, routes_turns).reshape((TOKENS, TOP))
    gates = jnp.clip(jnp.exp(math.log(1.0) - 2.3025851 * jax.random.uniform(keys[3], (TOKENS, TOP), jnp.float32) ** steps_of(keys[3], (TOKENS, TOP), ((0, 128),), -0.2, 0.2)), 0.1, 1.0)
    w_gate = normal_values(keys[4], (EXPERTS, D, FF), D ** -0.5, 0.09375, ((0, 64), (1, 8)))
    w_up = normal_values(keys[5], (EXPERTS, D, FF), D ** -0.5, 0.09375, ((0, 64), (1, 8)))
    w_down = normal_values(keys[6], (EXPERTS, FF, D), FF ** -0.5, 0.1875, ((0, 64), (2, 8)))
    return dict(tokens=tokens, cotangent=cotangent, routes=routes, gates=gates, w_gate=w_gate, w_up=w_up, w_down=w_down)


def silu_parts(value):
    sig = jax.nn.sigmoid(value)
    return value * sig, sig * (1.0 + value * (1.0 - sig))


def contract_rows(left, right):
    return lax.dot_general(left, right, (((0,), (0,)), ((), ())), preferred_element_type=jnp.float32)


def contract_cols(left, right):
    return lax.dot_general(left, right, (((1,), (1,)), ((), ())), preferred_element_type=jnp.float32)


def reference(tokens, cotangent, routes, gates, w_gate, w_up, w_down):
    flat = routes.reshape(-1).astype(jnp.int32)
    count = flat.shape[0]
    token_of = (jnp.arange(count, dtype=jnp.int32) // TOP).astype(jnp.int32)
    group_of = (token_of // TOK_DEV) % N_DP
    gflat = gates.reshape(-1)
    most_rows = N_EXPERT * N_DP * CAP
    zero_b = jnp.zeros((), jnp.bfloat16)

    def per_expert(carry, expert):
        mixed_acc, grad_acc = carry
        order = jnp.argsort((flat != expert).astype(jnp.int32), stable=True)[:most_rows].astype(jnp.int32)
        valid = flat[order] == expert
        rows_tok = token_of[order]
        rows_x = jnp.where(valid[:, None], tokens[rows_tok], zero_b)
        rows_g = jnp.where(valid, gflat[order], jnp.zeros((), jnp.float32))
        out_grad = (rows_g[:, None] * cotangent[rows_tok].astype(jnp.float32)).astype(jnp.bfloat16)
        wg = w_gate[expert]
        wu = w_up[expert]
        wd = w_down[expert]
        gate_pre = jnp.dot(rows_x, wg, preferred_element_type=jnp.float32)
        up_pre = jnp.dot(rows_x, wu, preferred_element_type=jnp.float32)
        act, slope = silu_parts(gate_pre)
        hidden = (act * up_pre).astype(jnp.bfloat16)
        expert_out = jnp.dot(hidden, wd, preferred_element_type=jnp.float32).astype(jnp.bfloat16)
        hidden_grad = contract_cols(out_grad, wd)
        gate_grad = (hidden_grad * up_pre * slope).astype(jnp.bfloat16)
        up_grad = (hidden_grad * act).astype(jnp.bfloat16)
        row_grad = (contract_cols(gate_grad, wg) + contract_cols(up_grad, wu)).astype(jnp.bfloat16)
        total_g = jnp.zeros(wg.shape, jnp.float32)
        total_u = jnp.zeros(wu.shape, jnp.float32)
        total_d = jnp.zeros(wd.shape, jnp.float32)
        for group in range(N_DP):
            inside = valid & (group_of[order] == group)
            part_x = jnp.where(inside[:, None], rows_x, zero_b)
            part_h = jnp.where(inside[:, None], hidden, zero_b)
            total_g = total_g + contract_rows(part_x, gate_grad).astype(jnp.bfloat16).astype(jnp.float32)
            total_u = total_u + contract_rows(part_x, up_grad).astype(jnp.bfloat16).astype(jnp.float32)
            total_d = total_d + contract_rows(part_h, out_grad).astype(jnp.bfloat16).astype(jnp.float32)
        mixed_add = jnp.where(valid[:, None], rows_g[:, None] * expert_out.astype(jnp.float32), jnp.zeros((), jnp.float32))
        grad_add = jnp.where(valid[:, None], row_grad.astype(jnp.float32), jnp.zeros((), jnp.float32))
        mixed_acc = mixed_acc.at[rows_tok].add(mixed_add)
        grad_acc = grad_acc.at[rows_tok].add(grad_add)
        return (mixed_acc, grad_acc), (total_g.astype(jnp.bfloat16), total_u.astype(jnp.bfloat16), total_d.astype(jnp.bfloat16))

    start = (jnp.zeros(tokens.shape, jnp.float32), jnp.zeros(tokens.shape, jnp.float32))
    (mixed, token_grad), (grad_gate, grad_up, grad_down) = lax.scan(per_expert, start, jnp.arange(EXPERTS, dtype=jnp.int32))
    return mixed.astype(jnp.bfloat16), token_grad.astype(jnp.bfloat16), grad_gate, grad_up, grad_down
```

```python
import functools

import jax
import jax.numpy as jnp
from jax import lax
from jax.experimental import pallas as pl
from jax.experimental.pallas import tpu as pltpu
from jax.sharding import PartitionSpec as P

CAP = 3
CHIPS = 4
MESH = pl.DeviceIdType.MESH
BF16, F32 = jnp.bfloat16, jnp.float32


def dot(left, right):
    return lax.dot_general(left, right, (((1,), (0,)), ((), ())), preferred_element_type=F32)


def dot_rows(left, right):
    return lax.dot_general(left, right, (((0,), (0,)), ((), ())), preferred_element_type=F32)


def dot_cols(left, right):
    return lax.dot_general(left, right, (((1,), (1,)), ((), ())), preferred_element_type=F32)


def silu_parts(value):
    sig = 1.0 / (1.0 + jnp.exp(-value))
    return value * sig, sig * (1.0 + value * (1.0 - sig))


def iota(shape, dim):
    return lax.broadcasted_iota(jnp.int32, shape, dim)


def kernel(
    side, tok_ref, cot_ref, routes_ref, gates_ref, wg_hbm, wu_hbm, wd_hbm,
    mixed_ref, grad_ref, gg_ref, gu_ref, gd_ref,
    wg, wu, wd, tokbuf, metabuf, cmat, perm, send2, recv2, x_ref, do_ref, pair_send, pair_recv, mine,
    far_send, far_recv, imm_send, imm_recv, sum_send, sum_recv, act, send3, recv3, send4, recv4,
    w_sem, s1, r1, s1m, r1m, s2, r2, sp, rp, sy, ry, s5, r5, s3, r3, s4, r4,
):
    toks, piece = tok_ref.shape
    top = routes_ref.shape[1]
    lanes = side * toks
    block = side * CAP
    rows = 2 * side * block
    chunk = rows // (2 * CHIPS)
    half = wg.shape[1] // 2

    p, e, d = lax.axis_index("pipe"), lax.axis_index("expert"), lax.axis_index("dp")
    c, j = lax.rem(p, 2), lax.div(p, 2)
    hi, lo = lax.div(e, side), lax.rem(e, side)
    a, b = hi * (1 - c) + lo * c, lo * (1 - c) + hi * c
    sa, sb = side * (1 - c) + c, (1 - c) + side * c
    up, dn, far = lax.rem(j + 1, CHIPS), lax.rem(j + CHIPS - 1, CHIPS), lax.rem(j + 2, CHIPS)
    sib_dev = (2 * j + 1 - c, e, d)
    up_dev = (2 * up + c, e, d)
    dn_dev = (2 * dn + c, e, d)

    def a_dev(i):
        return (p, lax.rem(a + i, side) * sa + b * sb, d)

    def b_dev(i, dd):
        return (p, a * sa + lax.rem(b + i, side) * sb, lax.rem(d + dd, 2))

    b_peers = [(i, dd) for dd in range(2) for i in range(side) if i or dd]

    barrier = pltpu.get_barrier_semaphore()
    peers = [a_dev(i) for i in range(1, side)] + [b_dev(i, dd) for i, dd in b_peers]
    peers += [sib_dev, up_dev, dn_dev]
    for dev in peers:
        pl.semaphore_signal(barrier, inc=1, device_id=dev, device_id_type=MESH)

    width = wg.shape[1]
    off = pl.multiple_of(d * width, width)
    loads = [
        pltpu.make_async_copy(wg_hbm.at[0, :, pl.ds(off, width)], wg, w_sem.at[0]),
        pltpu.make_async_copy(wu_hbm.at[0, :, pl.ds(off, width)], wu, w_sem.at[1]),
        pltpu.make_async_copy(wd_hbm.at[0, pl.ds(off, width), :], wd, w_sem.at[2]),
    ]
    for load in loads:
        load.start()

    started = []

    def send(src, dst, ssem, rsem, dev):
        copy = pltpu.make_async_remote_copy(
            src_ref=src, dst_ref=dst, send_sem=ssem, recv_sem=rsem, device_id=dev, device_id_type=MESH
        )
        copy.start()
        started.append(copy)
        return copy

    tokbuf[a, 0:toks, :] = tok_ref[...]
    tokbuf[a, toks:, :] = cot_ref[...]
    lane = iota((toks, lanes), 1)
    own = (lax.rem(lane, toks) == iota((toks, lanes), 0)) & (lax.div(lane, toks) == a)
    meta = []
    for values in (routes_ref[...].astype(F32), gates_ref[...]):
        for k in range(top):
            spread = jnp.broadcast_to(values[:, k : k + 1], (toks, lanes))
            meta.append(jnp.sum(jnp.where(own, spread, 0.0), axis=0, keepdims=True))
    metabuf[a] = jnp.concatenate(meta, axis=0)

    size = 2 * side * block
    to, frm = iota((size, size), 0), iota((size, size), 1)
    to_kind, to = lax.div(to, side * block), lax.rem(to, side * block)
    to_x, to_slot, to_z = lax.div(to, block), lax.div(lax.rem(to, block), side), lax.rem(to, side)
    frm_b, frm = lax.div(frm, 2 * block), lax.rem(frm, 2 * block)
    frm_kind, frm = lax.div(frm, block), lax.rem(frm, block)
    frm_slot, frm_a = lax.div(frm, side), lax.rem(frm, side)
    same = (to_kind == frm_kind) & (to_slot == frm_slot)
    same = same & (frm_b == to_x * (1 - c) + to_z * c) & (frm_a == to_z * (1 - c) + to_x * c)
    perm[...] = jnp.where(same, 1.0, 0.0).astype(BF16)

    pl.semaphore_wait(barrier, len(peers))

    gather = []
    for i in range(1, side):
        gather.append(send(metabuf.at[a], metabuf.at[a], s1m.at[i], r1m.at[i], a_dev(i)))
    for i in range(1, side):
        gather.append(send(tokbuf.at[a], tokbuf.at[a], s1.at[i], r1.at[i], a_dev(i)))
    for copy in gather[: side - 1]:
        copy.wait_recv()

    total = metabuf[0]
    for i in range(1, side):
        total = total + metabuf[i]
    routes, gates = total[:top], total[top:]
    named, weights = [], []
    for i in range(side):
        hit = routes == (a * sa + i * sb).astype(F32)
        named.append(jnp.sum(jnp.where(hit, 1.0, 0.0), axis=0, keepdims=True))
        weights.append(jnp.sum(jnp.where(hit, gates, 0.0), axis=0, keepdims=True))
    first, second = iota((lanes, lanes), 0), iota((lanes, lanes), 1)
    earlier = (lax.div(first, toks) == lax.div(second, toks)) & (first < second)
    before = dot(
        jnp.concatenate(named, axis=0).astype(BF16), jnp.where(earlier, 1.0, 0.0).astype(BF16)
    )
    slot, source = iota((block, lanes), 0), iota((block, lanes), 1)
    here = lax.rem(slot, side) == lax.div(source, toks)
    slot = lax.div(slot, side).astype(F32)
    picks, scales = [], []
    empty = jnp.zeros((block, lanes), F32)
    for i in range(side):
        pick = jnp.where(here & (before[i : i + 1] == slot) & (named[i] > 0.5), 1.0, 0.0)
        scaled = pick * weights[i]
        picks.append(pick)
        scales.append(jnp.sum(scaled, axis=1, keepdims=True))
        high = scaled.astype(BF16).astype(F32)
        low = scaled - high
        wide = jnp.concatenate(
            [
                jnp.concatenate([high, low, empty], axis=1),
                jnp.concatenate([empty, empty, pick], axis=1),
            ],
            axis=0,
        )
        cmat[2 * block * i : 2 * block * (i + 1), :] = wide.astype(BF16)
    place = jnp.concatenate(picks, axis=0).astype(BF16)
    scale = jnp.concatenate(scales, axis=0)

    for copy in gather[side - 1 :]:
        copy.wait_recv()
    xr = dot(place, tokbuf[:, 0:toks, :].reshape(lanes, piece))
    dr = dot(place, tokbuf[:, toks:, :].reshape(lanes, piece)) * scale
    for i in range(side):
        part = slice(block * i, block * (i + 1))
        send2[i] = jnp.concatenate([xr[part], dr[part]], axis=0).astype(BF16)
    copies = []
    for i, dd in b_peers:
        k = dd * side + i
        copies.append(send(send2.at[lax.rem(b + i, side)], recv2.at[d, b], s2.at[k], r2.at[k], b_dev(i, dd)))
    recv2[d, b] = send2[b]
    for load in loads:
        load.wait()
    for copy in copies:
        copy.wait_recv()

    for g in range(2):
        sorted_rows = dot(perm[...], recv2[g].reshape(2 * side * block, piece)).astype(BF16)
        x_ref[g * side * block : (g + 1) * side * block, :] = sorted_rows[: side * block]
        do_ref[g * side * block : (g + 1) * side * block, :] = sorted_rows[side * block :]

    def rows_of(ref, core):
        return jnp.concatenate(
            [ref[pl.ds(pl.multiple_of((2 * k + core) * chunk, chunk), chunk), :] for k in range(CHIPS)], axis=0
        )

    def partials(core, out, cast, after):
        xs, ds = rows_of(x_ref, core), rows_of(do_ref, core)
        for h in range(2):
            cols = slice(h * half, (h + 1) * half)
            for q, value in enumerate((dot(xs, wg[:, cols]), dot(xs, wu[:, cols]), dot_cols(ds, wd[cols, :]))):
                for k in range(CHIPS):
                    out[h, k, q * chunk : (q + 1) * chunk, :] = value[k * chunk : (k + 1) * chunk].astype(cast)
            after(h)

    pair = []
    partials(
        1 - c, pair_send, BF16,
        lambda h: pair.append(send(pair_send.at[h], pair_recv.at[h], sp.at[h], rp.at[h], sib_dev)),
    )
    partials(c, mine, F32, lambda h: None)

    def chip_sum(h, k):
        return mine[h, k] + pair_recv[h, k].astype(F32)

    ring = ((up, up_dev, dn, dn_dev), (dn, dn_dev, up, up_dev))
    fars, imms, sums = [], [], []
    for h in range(2):
        on, on_dev, back, back_dev = ring[h]
        pair[h].wait_recv()
        far_send[h] = chip_sum(h, far).astype(BF16)
        fars.append(send(far_send.at[h], far_recv.at[h], sy.at[h], ry.at[h], on_dev))
        imm_send[h] = chip_sum(h, back).astype(BF16)
        imms.append(send(imm_send.at[h], imm_recv.at[h], sy.at[2 + h], ry.at[2 + h], back_dev))
    for h in range(2):
        on, on_dev, back, back_dev = ring[h]
        fars[h].wait_recv()
        sum_send[h] = (chip_sum(h, on) + far_recv[h].astype(F32)).astype(BF16)
        sums.append(send(sum_send.at[h], sum_recv.at[h], sy.at[4 + h], ry.at[4 + h], on_dev))

    ups, dns, sibs = [], [], []
    for h in range(2):
        imms[h].wait_recv()
        sums[h].wait_recv()
        pre = chip_sum(h, j) + imm_recv[h].astype(F32) + sum_recv[h].astype(F32)
        gate, upv, hid_grad = pre[:chunk], pre[chunk : 2 * chunk], pre[2 * chunk :]
        silu, slope = silu_parts(gate)
        act[j, c, h, 0:chunk, :] = (silu * upv).astype(BF16)
        act[j, c, h, chunk : 2 * chunk, :] = (hid_grad * upv * slope).astype(BF16)
        act[j, c, h, 2 * chunk :, :] = (hid_grad * silu).astype(BF16)
        own_piece = act.at[j, c, h]
        ups.append(send(own_piece, own_piece, s5.at[h], r5.at[h], up_dev))
        dns.append(send(own_piece, own_piece, s5.at[2 + h], r5.at[2 + h], dn_dev))
        sibs.append(send(own_piece, own_piece, s5.at[6 + h], r5.at[6 + h], sib_dev))
    ups[0].wait_recv()
    below = act.at[dn, c, 0]
    far0 = send(below, below, s5.at[4], r5.at[4], up_dev)
    dns[1].wait_recv()
    above = act.at[up, c, 1]
    far1 = send(above, above, s5.at[5], r5.at[5], dn_dev)
    sibs.append(send(below, below, s5.at[8], r5.at[8], sib_dev))
    sibs.append(send(above, above, s5.at[9], r5.at[9], sib_dev))
    ups[1].wait_recv()
    piece1 = act.at[dn, c, 1]
    sibs.append(send(piece1, piece1, s5.at[10], r5.at[10], sib_dev))
    dns[0].wait_recv()
    piece0 = act.at[up, c, 0]
    sibs.append(send(piece0, piece0, s5.at[11], r5.at[11], sib_dev))
    for h, copy in enumerate((far0, far1)):
        copy.wait_recv()
        piece2 = act.at[far, c, h]
        sibs.append(send(piece2, piece2, s5.at[12 + h], r5.at[12 + h], sib_dev))
    for copy in sibs:
        copy.wait_recv()

    def gathered(q):
        part = slice(q * chunk, (q + 1) * chunk)
        return jnp.concatenate(
            [
                jnp.concatenate([act[k, core, 0, part, :], act[k, core, 1, part, :]], axis=1)
                for k in range(CHIPS)
                for core in range(2)
            ],
            axis=0,
        )

    hidden, gate_grad, up_grad = gathered(0), gathered(1), gathered(2)
    outs = dot(hidden, wd[...])
    row_grads = dot_cols(gate_grad, wg[...]) + dot_cols(up_grad, wu[...])
    for g in range(2):
        part = slice(g * side * block, (g + 1) * side * block)
        stacked = jnp.concatenate([outs[part], row_grads[part]], axis=0).astype(BF16)
        send3[g] = dot_rows(perm[...], stacked).astype(BF16).reshape(side, 2 * block, piece)
    copies = []
    for i, dd in b_peers:
        k = dd * side + i
        copies.append(
            send(
                send3.at[lax.rem(d + dd, 2), lax.rem(b + i, side)], recv3.at[d, b], s3.at[k], r3.at[k], b_dev(i, dd)
            )
        )
    recv3[d, b] = send3[d, b]

    gg_ref[0] = dot_rows(x_ref[...], gate_grad).astype(BF16)
    gu_ref[0] = dot_rows(x_ref[...], up_grad).astype(BF16)
    gd_ref[0] = dot_rows(hidden, do_ref[...]).astype(BF16)

    for copy in copies:
        copy.wait_recv()
    both = dot_rows(cmat[...], recv3[0].reshape(2 * side * block, piece))
    both = both + dot_rows(cmat[...], recv3[1].reshape(2 * side * block, piece))
    part_mixed = both[:lanes] + both[lanes : 2 * lanes]
    part_grad = both[2 * lanes :]
    for i in range(side):
        part = slice(i * toks, (i + 1) * toks)
        send4[i] = jnp.concatenate([part_mixed[part], part_grad[part]], axis=0).astype(BF16)
    copies = []
    for i in range(1, side):
        copies.append(send(send4.at[lax.rem(a + i, side)], recv4.at[a], s4.at[i], r4.at[i], a_dev(i)))
    recv4[a] = send4[a]
    for copy in copies:
        copy.wait_recv()
    final = recv4[0].astype(F32)
    for i in range(1, side):
        final = final + recv4[i].astype(F32)
    mixed_ref[...] = final[:toks].astype(BF16)
    grad_ref[...] = final[toks:].astype(BF16)
    for copy in started:
        copy.wait_send()


def on_device(side, tokens, cotangent, routes, gates, w_gate, w_up, w_down):
    toks, piece = tokens.shape
    top = routes.shape[1]
    width = w_gate.shape[2] // 2
    half = width // 2
    lanes = side * toks
    block = side * CAP
    rows = 2 * side * block
    chunk = rows // (2 * CHIPS)
    vmem = pl.BlockSpec(memory_space=pltpu.VMEM)
    hbm = pl.BlockSpec(memory_space=pl.ANY)
    dma = pltpu.SemaphoreType.DMA
    quarter = (2, 3 * chunk, half)
    return pl.pallas_call(
        functools.partial(kernel, side),
        out_shape=(
            jax.ShapeDtypeStruct((toks, piece), BF16),
            jax.ShapeDtypeStruct((toks, piece), BF16),
            jax.ShapeDtypeStruct((1, piece, width), BF16),
            jax.ShapeDtypeStruct((1, piece, width), BF16),
            jax.ShapeDtypeStruct((1, width, piece), BF16),
        ),
        in_specs=[vmem] * 4 + [hbm] * 3,
        out_specs=(vmem,) * 5,
        scratch_shapes=[
            pltpu.VMEM((piece, width), BF16),
            pltpu.VMEM((piece, width), BF16),
            pltpu.VMEM((width, piece), BF16),
            pltpu.VMEM((side, 2 * toks, piece), BF16),
            pltpu.VMEM((side, 2 * top, lanes), F32),
            pltpu.VMEM((2 * side * block, 3 * lanes), BF16),
            pltpu.VMEM((2 * side * block, 2 * side * block), BF16),
            pltpu.VMEM((side, 2 * block, piece), BF16),
            pltpu.VMEM((2, side, 2 * block, piece), BF16),
            pltpu.VMEM((rows, piece), BF16),
            pltpu.VMEM((rows, piece), BF16),
            pltpu.VMEM((2, CHIPS, 3 * chunk, half), BF16),
            pltpu.VMEM((2, CHIPS, 3 * chunk, half), BF16),
            pltpu.VMEM((2, CHIPS, 3 * chunk, half), F32),
            pltpu.VMEM(quarter, BF16),
            pltpu.VMEM(quarter, BF16),
            pltpu.VMEM(quarter, BF16),
            pltpu.VMEM(quarter, BF16),
            pltpu.VMEM(quarter, BF16),
            pltpu.VMEM(quarter, BF16),
            pltpu.VMEM((CHIPS, 2, 2, 3 * chunk, half), BF16),
            pltpu.VMEM((2, side, 2 * block, piece), BF16),
            pltpu.VMEM((2, side, 2 * block, piece), BF16),
            pltpu.VMEM((side, 2 * toks, piece), BF16),
            pltpu.VMEM((side, 2 * toks, piece), BF16),
            dma((3,)),
            dma((side,)), dma((side,)), dma((side,)), dma((side,)),
            dma((2 * side,)), dma((2 * side,)),
            dma((2,)), dma((2,)),
            dma((6,)), dma((6,)),
            dma((14,)), dma((14,)),
            dma((2 * side,)), dma((2 * side,)),
            dma((side,)), dma((side,)),
        ],
        compiler_params=pltpu.CompilerParams(
            collective_id=0, has_side_effects=True, vmem_limit_bytes=40 * 1024 * 1024
        ),
        cost_estimate=pl.CostEstimate(
            flops=16 * rows * piece * width, bytes_accessed=6 * piece * width * 2, transcendentals=0
        ),
    )(tokens, cotangent, routes, gates, w_gate, w_up, w_down)


def solution(mesh):
    experts = mesh.shape["expert"]
    side = next(s for s in range(1, experts + 1) if s * s == experts)
    in_specs = (
        P(("expert", "dp"), "pipe"),
        P(("expert", "dp"), "pipe"),
        P(("expert", "dp"), None),
        P(("expert", "dp"), None),
        P("expert", "pipe", None),
        P("expert", "pipe", None),
        P("expert", None, "pipe"),
    )
    out_specs = (
        P(("expert", "dp"), "pipe"),
        P(("expert", "dp"), "pipe"),
        P("expert", "pipe", "dp"),
        P("expert", "pipe", "dp"),
        P("expert", "dp", "pipe"),
    )
    return jax.shard_map(
        functools.partial(on_device, side), mesh=mesh, in_specs=in_specs, out_specs=out_specs, check_vma=False
    )
```

```python
import functools

import jax
import jax.numpy as jnp
from jax import lax
from jax.experimental import pallas as pl
from jax.experimental.pallas import tpu as pltpu
from jax.sharding import PartitionSpec as P

CAP = 3
CHIPS = 4
VMEM_LIMIT = 60 * 1024 * 1024
MESH = pl.DeviceIdType.MESH
BF16, F32 = jnp.bfloat16, jnp.float32


def dot(left, right):
    return lax.dot_general(left, right, (((1,), (0,)), ((), ())), preferred_element_type=F32)


def dot_rows(left, right):
    return lax.dot_general(left, right, (((0,), (0,)), ((), ())), preferred_element_type=F32)


def dot_cols(left, right):
    return lax.dot_general(left, right, (((1,), (1,)), ((), ())), preferred_element_type=F32)


def silu_parts(value):
    sig = 1.0 / (1.0 + jnp.exp(-value))
    return value * sig, sig * (1.0 + value * (1.0 - sig))


def iota(shape, dim):
    return lax.broadcasted_iota(jnp.int32, shape, dim)


def kernel(
    side, tok_ref, cot_ref, routes_ref, gates_ref, wg_hbm, wu_hbm, wd_hbm,
    mixed_out, grad_out, gg_out, gu_out, gd_out,
    routes_vmem, gates_vmem, mixed_ref, grad_ref, gg_ref, gu_ref, gd_ref, in_sem, out_sem, wg, wu, wd,
    tokbuf, metabuf, cmat, perm, perm_back, send2, recv2, x_ref, do_ref, pair_send, pair_recv, mine,
    far_send, far_recv, imm_send, imm_recv, sum_send, sum_recv, act, send3, recv3, send4, recv4,
    w_sem, s1, r1, s1m, r1m, s2, r2, sp, rp, sy, ry, s5, r5, s3, r3, s4, r4,
):
    toks, piece = tok_ref.shape
    top = routes_ref.shape[0]
    lanes = side * toks
    block = side * CAP
    rows = side * block
    size = 2 * rows
    width = wg.shape[1]
    cols = width // CHIPS
    part = rows // 4

    p, e, d = lax.axis_index("pipe"), lax.axis_index("expert"), lax.axis_index("dp")
    c, j = lax.rem(p, 2), lax.div(p, 2)
    hi, lo = lax.div(e, side), lax.rem(e, side)
    a, b = hi * (1 - c) + lo * c, lo * (1 - c) + hi * c
    sa, sb = side * (1 - c) + c, (1 - c) + side * c
    up, dn, far = lax.rem(j + 1, CHIPS), lax.rem(j + CHIPS - 1, CHIPS), lax.rem(j + 2, CHIPS)
    sib_dev = (2 * j + 1 - c, e, d)
    up_dev = (2 * up + c, e, d)
    dn_dev = (2 * dn + c, e, d)

    def a_dev(i):
        return (p, lax.rem(a + i, side) * sa + b * sb, d)

    def b_dev(i, s):
        return (p, a * sa + lax.rem(b + i, side) * sb, lax.rem(d + s, 2))

    b_peers = [[i for i in range(side) if i or s] for s in range(2)]

    barrier = pltpu.get_barrier_semaphore()
    peers = [a_dev(i) for i in range(1, side)] + [b_dev(i, s) for s in range(2) for i in b_peers[s]]
    peers += [sib_dev, up_dev, dn_dev]
    for dev in peers:
        pl.semaphore_signal(barrier, inc=1, device_id=dev, device_id_type=MESH)

    inputs = [
        pltpu.make_async_copy(routes_ref, routes_vmem, in_sem.at[0]),
        pltpu.make_async_copy(gates_ref, gates_vmem, in_sem.at[1]),
        pltpu.make_async_copy(tok_ref, tokbuf.at[a, pl.ds(0, toks)], in_sem.at[2]),
        pltpu.make_async_copy(cot_ref, tokbuf.at[a, pl.ds(toks, toks)], in_sem.at[3]),
    ]
    for load in inputs:
        load.start()
    off = pl.multiple_of(d * width, width)
    loads = [
        pltpu.make_async_copy(wg_hbm.at[0, :, pl.ds(off, width)], wg, w_sem.at[0]),
        pltpu.make_async_copy(wu_hbm.at[0, :, pl.ds(off, width)], wu, w_sem.at[1]),
        pltpu.make_async_copy(wd_hbm.at[0, pl.ds(off, width), :], wd, w_sem.at[2]),
    ]
    for load in loads:
        load.start()

    started = []

    def send(src, dst, ssem, rsem, dev):
        copy = pltpu.make_async_remote_copy(
            src_ref=src, dst_ref=dst, send_sem=ssem, recv_sem=rsem, device_id=dev, device_id_type=MESH
        )
        copy.start()
        started.append(copy)
        return copy

    own = lax.div(iota((2 * top, lanes), 1), toks) == a
    for load in inputs:
        load.wait()
    values = jnp.concatenate([routes_vmem[...].astype(F32), gates_vmem[...]], axis=0)
    metabuf[a] = jnp.where(own, jnp.concatenate([values] * side, axis=1), 0.0)

    pl.semaphore_wait(barrier, len(peers))

    gather = []
    for i in range(1, side):
        gather.append(send(metabuf.at[a], metabuf.at[a], s1m.at[i], r1m.at[i], a_dev(i)))
    for i in range(1, side):
        gather.append(send(tokbuf.at[a], tokbuf.at[a], s1.at[i], r1.at[i], a_dev(i)))

    def sorted_place(at):
        at_b, at = lax.div(at, 2 * block), lax.rem(at, 2 * block)
        kind, at = lax.div(at, block), lax.rem(at, block)
        slot, at_a = lax.div(at, side), lax.rem(at, side)
        at_x, at_z = at_b * (1 - c) + at_a * c, at_a * (1 - c) + at_b * c
        return kind * rows + at_x * block + slot * side + at_z

    perm[...] = jnp.where(iota((size, size), 0) == sorted_place(iota((1, size), 1)), 1.0, 0.0).astype(BF16)
    perm_back[...] = jnp.where(iota((size, size), 1) == sorted_place(iota((size, 1), 0)), 1.0, 0.0).astype(BF16)
    first, second = iota((lanes, lanes), 0), iota((lanes, lanes), 1)
    earlier = (lax.div(first, toks) == lax.div(second, toks)) & (first < second)
    earlier = jnp.where(earlier, 1.0, 0.0).astype(BF16)
    slot, source = iota((block, lanes), 0), iota((block, lanes), 1)
    here = lax.rem(slot, side) == lax.div(source, toks)
    slot = lax.div(slot, side).astype(F32)

    for copy in gather[: side - 1]:
        copy.wait_recv()

    total = metabuf[0]
    for i in range(1, side):
        total = total + metabuf[i]
    routes, gates = total[:top], total[top:]
    named, weights = [], []
    for i in range(side):
        hit = routes == (a * sa + i * sb).astype(F32)
        named.append(jnp.sum(jnp.where(hit, 1.0, 0.0), axis=0, keepdims=True))
        weights.append(jnp.sum(jnp.where(hit, gates, 0.0), axis=0, keepdims=True))
    before = dot(jnp.concatenate(named, axis=0).astype(BF16), earlier)
    picks, scales = [], []
    for i in range(side):
        pick = jnp.where(here & (before[i : i + 1] == slot) & (named[i] > 0.5), 1.0, 0.0)
        picks.append(pick)
        scales.append(jnp.sum(pick * weights[i], axis=1, keepdims=True))
    place = jnp.concatenate(picks, axis=0).astype(BF16)
    scale = jnp.concatenate(scales, axis=0)

    for copy in gather[side - 1 :]:
        copy.wait_recv()
    xr = dot(place, tokbuf[:, 0:toks, :].reshape(lanes, piece))
    dr = dot(place, tokbuf[:, toks:, :].reshape(lanes, piece)) * scale
    for i in range(side):
        at = slice(block * i, block * (i + 1))
        send2[i] = jnp.concatenate([xr[at], dr[at]], axis=0).astype(BF16)
    to_experts = [[], []]
    for s in range(2):
        for i in b_peers[s]:
            to_experts[s].append(
                send(send2.at[lax.rem(b + i, side)], recv2.at[s, b], s2.at[s, i], r2.at[s, i], b_dev(i, s))
            )
    recv2[0, b] = send2[b]

    empty = jnp.zeros((block, lanes), F32)
    wide = []
    for i in range(side):
        scaled = picks[i] * weights[i]
        high = scaled.astype(BF16).astype(F32)
        wide.append(jnp.concatenate([high, scaled - high, empty], axis=1))
        wide.append(jnp.concatenate([empty, empty, picks[i]], axis=1))
    cmat[...] = jnp.concatenate(wide, axis=0).T.astype(BF16)

    for load in loads:
        load.wait()

    pair, fars, imms, sums, ups, dns, sibs, relays = ([None, None] for _ in range(8))
    ring = ((up, up_dev, dn, dn_dev), (dn, dn_dev, up, up_dev))

    def partials(s, core, out, cast):
        at = pl.ds(pl.multiple_of(s * rows + core * 2 * part, 2 * part), 2 * part)
        xs, ds = x_ref[at, :], do_ref[at, :]
        for q, value in enumerate((dot(xs, wg[...]), dot(xs, wu[...]), dot_cols(ds, wd[...]))):
            for h in range(2):
                for k in range(CHIPS):
                    out[s, h, k, q * part : (q + 1) * part, :] = value[
                        h * part : (h + 1) * part, k * cols : (k + 1) * cols
                    ].astype(cast)

    def project(s):
        for copy in to_experts[s]:
            copy.wait_recv()
        found = dot(perm[...], recv2[s].reshape(size, piece)).astype(BF16)
        x_ref[s * rows : (s + 1) * rows, :] = found[:rows]
        do_ref[s * rows : (s + 1) * rows, :] = found[rows:]
        partials(s, 1 - c, pair_send, BF16)
        pair[s] = send(pair_send.at[s], pair_recv.at[s], sp.at[s], rp.at[s], sib_dev)
        partials(s, c, mine, F32)

    def chip_sum(s, h, k):
        return mine[s, h, k] + pair_recv[s, h, k].astype(F32)

    def scatter_start(s):
        fars[s], imms[s] = [], []
        pair[s].wait_recv()
        for h in range(2):
            far_send[s, h] = chip_sum(s, h, far).astype(BF16)
            fars[s].append(send(far_send.at[s, h], far_recv.at[s, h], sy.at[s, h], ry.at[s, h], ring[h][1]))
        for h in range(2):
            imm_send[s, h] = chip_sum(s, h, ring[h][2]).astype(BF16)
            imms[s].append(
                send(imm_send.at[s, h], imm_recv.at[s, h], sy.at[s, 2 + h], ry.at[s, 2 + h], ring[h][3])
            )

    def scatter_end(s):
        sums[s] = []
        for h in range(2):
            fars[s][h].wait_recv()
            sum_send[s, h] = (chip_sum(s, h, ring[h][0]) + far_recv[s, h].astype(F32)).astype(BF16)
            sums[s].append(
                send(sum_send.at[s, h], sum_recv.at[s, h], sy.at[s, 4 + h], ry.at[s, 4 + h], ring[h][1])
            )

    def pass_on(s, k, core, h, sem, dev):
        ref = act.at[s, k, core, h]
        return send(ref, ref, s5.at[s, sem], r5.at[s, sem], dev)

    def activate(s):
        ups[s], dns[s], sibs[s] = [], [], []
        for h in range(2):
            imms[s][h].wait_recv()
            sums[s][h].wait_recv()
            pre = chip_sum(s, h, j) + imm_recv[s, h].astype(F32) + sum_recv[s, h].astype(F32)
            gate, upv, hid_grad = pre[:part], pre[part : 2 * part], pre[2 * part :]
            silu, slope = silu_parts(gate)
            act[s, j, c, h, 0:part, :] = (silu * upv).astype(BF16)
            act[s, j, c, h, part : 2 * part, :] = (hid_grad * upv * slope).astype(BF16)
            act[s, j, c, h, 2 * part :, :] = (hid_grad * silu).astype(BF16)
            ups[s].append(pass_on(s, j, c, h, h, up_dev))
            dns[s].append(pass_on(s, j, c, h, 2 + h, dn_dev))
            sibs[s].append(pass_on(s, j, c, h, 6 + h, sib_dev))

    def relay(s):
        ups[s][0].wait_recv()
        relays[s] = [pass_on(s, dn, c, 0, 4, up_dev)]
        dns[s][1].wait_recv()
        relays[s].append(pass_on(s, up, c, 1, 5, dn_dev))
        sibs[s].append(pass_on(s, dn, c, 0, 8, sib_dev))
        sibs[s].append(pass_on(s, up, c, 1, 9, sib_dev))
        ups[s][1].wait_recv()
        sibs[s].append(pass_on(s, dn, c, 1, 10, sib_dev))
        dns[s][0].wait_recv()
        sibs[s].append(pass_on(s, up, c, 0, 11, sib_dev))

    def relay_end(s):
        for h in range(2):
            relays[s][h].wait_recv()
            sibs[s].append(pass_on(s, far, c, h, 12 + h, sib_dev))
        for copy in sibs[s]:
            copy.wait_recv()

    def gathered(s, q):
        at = slice(q * part, (q + 1) * part)
        return jnp.concatenate(
            [
                jnp.concatenate([act[s, k, core, h, at, :] for k in range(CHIPS)], axis=1)
                for core in range(2)
                for h in range(2)
            ],
            axis=0,
        )

    to_tokens = [[], []]

    def answer(s):
        outs = dot(gathered(s, 0), wd[...])
        row_grads = dot_cols(gathered(s, 1), wg[...]) + dot_cols(gathered(s, 2), wu[...])
        stacked = jnp.concatenate([outs, row_grads], axis=0).astype(BF16)
        send3[s] = dot(perm_back[...], stacked).astype(BF16).reshape(side, 2 * block, piece)
        for i in b_peers[s]:
            to_tokens[s].append(
                send(send3.at[s, lax.rem(b + i, side)], recv3.at[s, b], s3.at[s, i], r3.at[s, i], b_dev(i, s))
            )
        if s == 0:
            recv3[0, b] = send3[0, b]

    project(0)
    scatter_start(0)
    project(1)
    scatter_end(0)
    scatter_start(1)
    activate(0)
    scatter_end(1)
    relay(0)
    activate(1)
    relay_end(0)
    relay(1)
    answer(0)
    relay_end(1)
    answer(1)

    hidden, gate_grad, up_grad = (
        jnp.concatenate([gathered(0, q), gathered(1, q)], axis=0) for q in range(3)
    )
    stores = []
    for k, (ref, out, left, right) in enumerate(
        ((gg_ref, gg_out, x_ref[...], gate_grad), (gu_ref, gu_out, x_ref[...], up_grad), (gd_ref, gd_out, hidden, do_ref[...]))
    ):
        ref[...] = dot_rows(left, right).astype(BF16)
        stores.append(pltpu.make_async_copy(ref, out.at[0], out_sem.at[k]))
        stores[-1].start()

    both = None
    for s in range(2):
        for copy in to_tokens[s]:
            copy.wait_recv()
        value = dot(cmat[...], recv3[s].reshape(size, piece))
        both = value if both is None else both + value
    part_mixed = both[:lanes] + both[lanes : 2 * lanes]
    part_grad = both[2 * lanes :]
    for i in range(side):
        at = slice(i * toks, (i + 1) * toks)
        send4[i] = jnp.concatenate([part_mixed[at], part_grad[at]], axis=0).astype(BF16)
    home = []
    for i in range(1, side):
        home.append(send(send4.at[lax.rem(a + i, side)], recv4.at[a], s4.at[i], r4.at[i], a_dev(i)))
    recv4[a] = send4[a]
    for copy in home:
        copy.wait_recv()
    final = recv4[0].astype(F32)
    for i in range(1, side):
        final = final + recv4[i].astype(F32)
    mixed_ref[...] = final[:toks].astype(BF16)
    grad_ref[...] = final[toks:].astype(BF16)
    for k, (ref, out) in enumerate(((mixed_ref, mixed_out), (grad_ref, grad_out))):
        stores.append(pltpu.make_async_copy(ref, out, out_sem.at[3 + k]))
        stores[-1].start()
    for copy in stores:
        copy.wait()
    for copy in started:
        copy.wait_send()


def store(*refs):
    ins, outs, held, sems = refs[:5], refs[5:10], refs[10:15], refs[15]
    loads = [pltpu.make_async_copy(ins[i], held[i], sems.at[0, i]) for i in range(5)]
    stores = [pltpu.make_async_copy(held[i], outs[i], sems.at[1, i]) for i in range(5)]
    for load in loads:
        load.start()
    for load, copy in zip(loads, stores):
        load.wait()
        copy.start()
    for copy in stores:
        copy.wait()


def on_device(side, tokens, cotangent, routes, gates, w_gate, w_up, w_down):
    toks, piece = tokens.shape
    top = routes.shape[1]
    width = w_gate.shape[2] // 2
    lanes = side * toks
    block = side * CAP
    rows = side * block
    part = rows // 4
    hbm = pl.BlockSpec(memory_space=pltpu.MemorySpace.HBM)
    dma = pltpu.SemaphoreType.DMA
    halves = (2, 2, 3 * part, width // CHIPS)
    pieces = (2, 2, CHIPS, 3 * part, width // CHIPS)
    results = pl.pallas_call(
        functools.partial(kernel, side),
        out_shape=(
            jax.ShapeDtypeStruct((toks, piece), BF16),
            jax.ShapeDtypeStruct((toks, piece), BF16),
            jax.ShapeDtypeStruct((1, piece, width), BF16),
            jax.ShapeDtypeStruct((1, piece, width), BF16),
            jax.ShapeDtypeStruct((1, width, piece), BF16),
        ),
        in_specs=[hbm] * 7,
        out_specs=(hbm,) * 5,
        scratch_shapes=[
            pltpu.VMEM((top, toks), jnp.int32),
            pltpu.VMEM((top, toks), F32),
            pltpu.VMEM((toks, piece), BF16),
            pltpu.VMEM((toks, piece), BF16),
            pltpu.VMEM((piece, width), BF16),
            pltpu.VMEM((piece, width), BF16),
            pltpu.VMEM((width, piece), BF16),
            dma((4,)), dma((5,)),
            pltpu.VMEM((piece, width), BF16),
            pltpu.VMEM((piece, width), BF16),
            pltpu.VMEM((width, piece), BF16),
            pltpu.VMEM((side, 2 * toks, piece), BF16),
            pltpu.VMEM((side, 2 * top, lanes), F32),
            pltpu.VMEM((3 * lanes, 2 * rows), BF16),
            pltpu.VMEM((2 * rows, 2 * rows), BF16),
            pltpu.VMEM((2 * rows, 2 * rows), BF16),
            pltpu.VMEM((side, 2 * block, piece), BF16),
            pltpu.VMEM((2, side, 2 * block, piece), BF16),
            pltpu.VMEM((2 * rows, piece), BF16),
            pltpu.VMEM((2 * rows, piece), BF16),
            pltpu.VMEM(pieces, BF16),
            pltpu.VMEM(pieces, BF16),
            pltpu.VMEM(pieces, F32),
            pltpu.VMEM(halves, BF16),
            pltpu.VMEM(halves, BF16),
            pltpu.VMEM(halves, BF16),
            pltpu.VMEM(halves, BF16),
            pltpu.VMEM(halves, BF16),
            pltpu.VMEM(halves, BF16),
            pltpu.VMEM((2, CHIPS, 2, 2, 3 * part, width // CHIPS), BF16),
            pltpu.VMEM((2, side, 2 * block, piece), BF16),
            pltpu.VMEM((2, side, 2 * block, piece), BF16),
            pltpu.VMEM((side, 2 * toks, piece), BF16),
            pltpu.VMEM((side, 2 * toks, piece), BF16),
            dma((3,)),
            dma((side,)), dma((side,)), dma((side,)), dma((side,)),
            dma((2, side)), dma((2, side)),
            dma((2,)), dma((2,)),
            dma((2, 6)), dma((2, 6)),
            dma((2, 14)), dma((2, 14)),
            dma((2, side)), dma((2, side)),
            dma((side,)), dma((side,)),
        ],
        compiler_params=pltpu.CompilerParams(
            collective_id=0, has_side_effects=True, vmem_limit_bytes=VMEM_LIMIT
        ),
        cost_estimate=pl.CostEstimate(
            flops=32 * rows * piece * width, bytes_accessed=6 * piece * width * 2, transcendentals=0
        ),
    )(tokens, cotangent, routes.T, gates.T, w_gate, w_up, w_down)
    return pl.pallas_call(
        store,
        out_shape=[jax.ShapeDtypeStruct(value.shape, value.dtype) for value in results],
        in_specs=[hbm] * 5,
        out_specs=[hbm] * 5,
        scratch_shapes=[pltpu.VMEM(value.shape, value.dtype) for value in results] + [dma((2, 5))],
        compiler_params=pltpu.CompilerParams(vmem_limit_bytes=VMEM_LIMIT),
    )(*results)


def solution(mesh):
    experts = mesh.shape["expert"]
    side = next(s for s in range(1, experts + 1) if s * s == experts)
    in_specs = (
        P(("expert", "dp"), "pipe"),
        P(("expert", "dp"), "pipe"),
        P(("expert", "dp"), None),
        P(("expert", "dp"), None),
        P("expert", "pipe", None),
        P("expert", "pipe", None),
        P("expert", None, "pipe"),
    )
    out_specs = (
        P(("expert", "dp"), "pipe"),
        P(("expert", "dp"), "pipe"),
        P("expert", "pipe", "dp"),
        P("expert", "pipe", "dp"),
        P("expert", "dp", "pipe"),
    )
    return jax.shard_map(
        functools.partial(on_device, side), mesh=mesh, in_specs=in_specs, out_specs=out_specs, check_vma=False
    )
```

```python
import functools

import jax
import jax.numpy as jnp
from jax import lax
from jax.experimental import pallas as pl
from jax.experimental.pallas import tpu as pltpu
from jax.sharding import PartitionSpec as P

CAP = 3
CHIPS = 4
VMEM_LIMIT = 60 * 1024 * 1024
MESH = pl.DeviceIdType.MESH
BF16, F32 = jnp.bfloat16, jnp.float32


def dot(left, right):
    return lax.dot_general(left, right, (((1,), (0,)), ((), ())), preferred_element_type=F32)


def dot_rows(left, right):
    return lax.dot_general(left, right, (((0,), (0,)), ((), ())), preferred_element_type=F32)


def dot_cols(left, right):
    return lax.dot_general(left, right, (((1,), (1,)), ((), ())), preferred_element_type=F32)


def silu_parts(value):
    sig = 1.0 / (1.0 + jnp.exp(-value))
    return value * sig, sig * (1.0 + value * (1.0 - sig))


def iota(shape, dim):
    return lax.broadcasted_iota(jnp.int32, shape, dim)


def kernel(
    side, tok_ref, cot_ref, routes_ref, gates_ref, wg_hbm, wu_hbm, wd_hbm,
    mixed_out, grad_out, gg_out, gu_out, gd_out,
    routes_vmem, gates_vmem, mixed_ref, grad_ref, gg_ref, gu_ref, gd_ref, in_sem, out_sem, wg, wu, wd,
    tokbuf, metabuf, cmat, perm, perm_back, send2, recv2, x_ref, do_ref, pair_send, pair_recv, mine,
    far_send, far_recv, imm_send, imm_recv, sum_send, sum_recv, act, send3, recv3, send4, recv4, acc, other,
    w_sem, s1, r1, s1m, r1m, s2, r2, sp, rp, sy, ry, s5, r5, s3, r3, s4, r4, s6, r6,
):
    toks, piece = tok_ref.shape
    top = routes_ref.shape[0]
    lanes = side * toks
    block = side * CAP
    rows = side * block
    size = 2 * rows
    width = wg.shape[2]
    cols = width // CHIPS
    part = rows // 4

    p, e, d = lax.axis_index("pipe"), lax.axis_index("expert"), lax.axis_index("dp")
    c, j = lax.rem(p, 2), lax.div(p, 2)
    hi, lo = lax.div(e, side), lax.rem(e, side)
    a, b = hi * (1 - c) + lo * c, lo * (1 - c) + hi * c
    sa, sb = side * (1 - c) + c, (1 - c) + side * c
    up, dn, far = lax.rem(j + 1, CHIPS), lax.rem(j + CHIPS - 1, CHIPS), lax.rem(j + 2, CHIPS)
    sib_dev = (2 * j + 1 - c, e, d)
    up_dev = (2 * up + c, e, d)
    dn_dev = (2 * dn + c, e, d)

    def a_dev(i):
        return (p, lax.rem(a + i, side) * sa + b * sb, d)

    def b_dev(i, s):
        return (p, a * sa + lax.rem(b + i, side) * sb, lax.rem(d + s, 2))

    b_peers = [[i for i in range(side) if i or s] for s in range(2)]

    barrier = pltpu.get_barrier_semaphore()
    peers = [a_dev(i) for i in range(1, side)] + [b_dev(i, s) for s in range(2) for i in b_peers[s]]
    peers += [sib_dev, up_dev, dn_dev]
    for dev in peers:
        pl.semaphore_signal(barrier, inc=1, device_id=dev, device_id_type=MESH)

    inputs = [
        pltpu.make_async_copy(routes_ref, routes_vmem, in_sem.at[0]),
        pltpu.make_async_copy(gates_ref, gates_vmem, in_sem.at[1]),
        pltpu.make_async_copy(tok_ref, tokbuf.at[a, pl.ds(0, toks)], in_sem.at[2]),
        pltpu.make_async_copy(cot_ref, tokbuf.at[a, pl.ds(toks, toks)], in_sem.at[3]),
    ]
    for load in inputs:
        load.start()
    loads = []
    for s in range(2):
        off = pl.multiple_of((d * s + (1 - d) * (1 - s)) * width, width)
        for k, (src, dst) in enumerate(
            (
                (wg_hbm.at[0, :, pl.ds(off, width)], wg.at[s]),
                (wu_hbm.at[0, :, pl.ds(off, width)], wu.at[s]),
                (wd_hbm.at[0, pl.ds(off, width), :], wd.at[s]),
            )
        ):
            loads.append(pltpu.make_async_copy(src, dst, w_sem.at[s, k]))
    for load in loads:
        load.start()

    started = []

    def send(src, dst, ssem, rsem, dev):
        copy = pltpu.make_async_remote_copy(
            src_ref=src, dst_ref=dst, send_sem=ssem, recv_sem=rsem, device_id=dev, device_id_type=MESH
        )
        copy.start()
        started.append(copy)
        return copy

    own = lax.div(iota((2 * top, lanes), 1), toks) == a
    for load in inputs:
        load.wait()
    values = jnp.concatenate([routes_vmem[...].astype(F32), gates_vmem[...]], axis=0)
    metabuf[a] = jnp.where(own, jnp.concatenate([values] * side, axis=1), 0.0)

    pl.semaphore_wait(barrier, len(peers))

    gather = []
    for i in range(1, side):
        gather.append(send(metabuf.at[a], metabuf.at[a], s1m.at[i], r1m.at[i], a_dev(i)))
    for i in range(1, side):
        gather.append(send(tokbuf.at[a], tokbuf.at[a], s1.at[i], r1.at[i], a_dev(i)))

    def sorted_place(at):
        at_b, at = lax.div(at, 2 * block), lax.rem(at, 2 * block)
        kind, at = lax.div(at, block), lax.rem(at, block)
        slot, at_a = lax.div(at, side), lax.rem(at, side)
        at_x, at_z = at_b * (1 - c) + at_a * c, at_a * (1 - c) + at_b * c
        return kind * rows + at_x * block + slot * side + at_z

    perm[...] = jnp.where(iota((size, size), 0) == sorted_place(iota((1, size), 1)), 1.0, 0.0).astype(BF16)
    perm_back[...] = jnp.where(iota((size, size), 1) == sorted_place(iota((size, 1), 0)), 1.0, 0.0).astype(BF16)
    first, second = iota((lanes, lanes), 0), iota((lanes, lanes), 1)
    earlier = (lax.div(first, toks) == lax.div(second, toks)) & (first < second)
    earlier = jnp.where(earlier, 1.0, 0.0).astype(BF16)
    slot, source = iota((block, lanes), 0), iota((block, lanes), 1)
    here = lax.rem(slot, side) == lax.div(source, toks)
    slot = lax.div(slot, side).astype(F32)

    for copy in gather[: side - 1]:
        copy.wait_recv()

    total = metabuf[0]
    for i in range(1, side):
        total = total + metabuf[i]
    routes, gates = total[:top], total[top:]
    named, weights = [], []
    for i in range(side):
        hit = routes == (a * sa + i * sb).astype(F32)
        named.append(jnp.sum(jnp.where(hit, 1.0, 0.0), axis=0, keepdims=True))
        weights.append(jnp.sum(jnp.where(hit, gates, 0.0), axis=0, keepdims=True))
    before = dot(jnp.concatenate(named, axis=0).astype(BF16), earlier)
    picks, scales = [], []
    for i in range(side):
        pick = jnp.where(here & (before[i : i + 1] == slot) & (named[i] > 0.5), 1.0, 0.0)
        picks.append(pick)
        scales.append(jnp.sum(pick * weights[i], axis=1, keepdims=True))
    place = jnp.concatenate(picks, axis=0).astype(BF16)
    scale = jnp.concatenate(scales, axis=0)

    for copy in gather[side - 1 :]:
        copy.wait_recv()
    xr = dot(place, tokbuf[:, 0:toks, :].reshape(lanes, piece))
    dr = dot(place, tokbuf[:, toks:, :].reshape(lanes, piece)) * scale
    for i in range(side):
        at = slice(block * i, block * (i + 1))
        send2[i] = jnp.concatenate([xr[at], dr[at]], axis=0).astype(BF16)
    to_experts = [[], []]
    for s in range(2):
        for i in b_peers[s]:
            to_experts[s].append(
                send(send2.at[lax.rem(b + i, side)], recv2.at[s, b], s2.at[s, i], r2.at[s, i], b_dev(i, s))
            )
    recv2[0, b] = send2[b]

    empty = jnp.zeros((block, lanes), F32)
    wide = []
    for i in range(side):
        scaled = picks[i] * weights[i]
        high = scaled.astype(BF16).astype(F32)
        wide.append(jnp.concatenate([high, scaled - high, empty], axis=1))
        wide.append(jnp.concatenate([empty, empty, picks[i]], axis=1))
    cmat[...] = jnp.concatenate(wide, axis=0).T.astype(BF16)

    pair, fars, imms, sums, ups, dns, sibs, relays = ([None, None] for _ in range(8))
    ring = ((up, up_dev, dn, dn_dev), (dn, dn_dev, up, up_dev))

    def partials(s, core, out, cast):
        at = pl.ds(pl.multiple_of(core * 2 * part, 2 * part), 2 * part)
        xs, ds = x_ref[at, :], do_ref[at, :]
        for q, value in enumerate((dot(xs, wg[s]), dot(xs, wu[s]), dot_cols(ds, wd[s]))):
            for h in range(2):
                for k in range(CHIPS):
                    out[s, h, k, q * part : (q + 1) * part, :] = value[
                        h * part : (h + 1) * part, k * cols : (k + 1) * cols
                    ].astype(cast)

    def arrange(s):
        for copy in to_experts[s]:
            copy.wait_recv()
        found = dot(perm[...], recv2[s].reshape(size, piece)).astype(BF16)
        x_ref[s * rows : (s + 1) * rows, :] = found[:rows]
        do_ref[s * rows : (s + 1) * rows, :] = found[rows:]

    def project(s):
        partials(s, 1 - c, pair_send, BF16)
        pair[s] = send(pair_send.at[s], pair_recv.at[s], sp.at[s], rp.at[s], sib_dev)
        partials(s, c, mine, F32)

    def chip_sum(s, h, k):
        return mine[s, h, k] + pair_recv[s, h, k].astype(F32)

    def scatter_far(s):
        fars[s], imms[s] = [], []
        pair[s].wait_recv()
        for h in range(2):
            far_send[s, h] = chip_sum(s, h, far).astype(BF16)
            fars[s].append(send(far_send.at[s, h], far_recv.at[s, h], sy.at[s, h], ry.at[s, h], ring[h][1]))

    def scatter_near(s):
        for h in range(2):
            imm_send[s, h] = chip_sum(s, h, ring[h][2]).astype(BF16)
            imms[s].append(
                send(imm_send.at[s, h], imm_recv.at[s, h], sy.at[s, 2 + h], ry.at[s, 2 + h], ring[h][3])
            )

    def scatter_end(s):
        sums[s] = []
        for h in range(2):
            fars[s][h].wait_recv()
            sum_send[s, h] = (chip_sum(s, h, ring[h][0]) + far_recv[s, h].astype(F32)).astype(BF16)
            sums[s].append(
                send(sum_send.at[s, h], sum_recv.at[s, h], sy.at[s, 4 + h], ry.at[s, 4 + h], ring[h][1])
            )

    def pass_on(s, k, core, h, sem, dev):
        ref = act.at[s, core, k, h]
        return send(ref, ref, s5.at[s, sem], r5.at[s, sem], dev)

    def activate(s):
        ups[s], dns[s], sibs[s] = [], [], []
        for h in range(2):
            imms[s][h].wait_recv()
            sums[s][h].wait_recv()
            pre = chip_sum(s, h, j) + imm_recv[s, h].astype(F32) + sum_recv[s, h].astype(F32)
            gate, upv, hid_grad = pre[:part], pre[part : 2 * part], pre[2 * part :]
            silu, slope = silu_parts(gate)
            act[s, c, j, h, 0:part, :] = (silu * upv).astype(BF16)
            act[s, c, j, h, part : 2 * part, :] = (hid_grad * upv * slope).astype(BF16)
            act[s, c, j, h, 2 * part :, :] = (hid_grad * silu).astype(BF16)
            ups[s].append(pass_on(s, j, c, h, h, up_dev))
            dns[s].append(pass_on(s, j, c, h, 2 + h, dn_dev))
            sibs[s].append(pass_on(s, j, c, h, 6 + h, sib_dev))

    def relay(s):
        ups[s][0].wait_recv()
        relays[s] = [pass_on(s, dn, c, 0, 4, up_dev)]
        dns[s][1].wait_recv()
        relays[s].append(pass_on(s, up, c, 1, 5, dn_dev))
        sibs[s].append(pass_on(s, dn, c, 0, 8, sib_dev))
        sibs[s].append(pass_on(s, up, c, 1, 9, sib_dev))
        ups[s][1].wait_recv()
        sibs[s].append(pass_on(s, dn, c, 1, 10, sib_dev))
        dns[s][0].wait_recv()
        sibs[s].append(pass_on(s, up, c, 0, 11, sib_dev))

    def relay_end(s):
        for h in range(2):
            relays[s][h].wait_recv()
            sibs[s].append(pass_on(s, far, c, h, 12 + h, sib_dev))
        for copy in sibs[s]:
            copy.wait_recv()

    def gathered(ref, q):
        at = slice(q * part, (q + 1) * part)
        return jnp.concatenate(
            [
                jnp.concatenate([ref[core, k, h, at, :] for k in range(CHIPS)], axis=1)
                for core in range(2)
                for h in range(2)
            ],
            axis=0,
        )

    def answer(s):
        outs = dot(gathered(act.at[s], 0), wd[s])
        row_grads = dot_cols(gathered(act.at[s], 1), wg[s]) + dot_cols(gathered(act.at[s], 2), wu[s])
        return outs, row_grads

    arrange(0)
    for load in loads:
        load.wait()
    project(0)
    project(1)
    scatter_far(0)
    scatter_near(0)
    scatter_far(1)
    scatter_end(0)
    scatter_near(1)
    activate(0)
    scatter_end(1)
    relay(0)
    activate(1)
    relay_end(0)
    acc[0], acc[1] = answer(0)
    relay(1)
    swap = send(act.at[0, c], other.at[c], s6.at[0], r6.at[0], (p, e, 1 - d))
    relay_end(1)
    outs, row_grads = answer(1)
    stacked = jnp.concatenate([acc[0] + outs, acc[1] + row_grads], axis=0).astype(BF16)
    send3[...] = dot(perm_back[...], stacked).astype(BF16).reshape(side, 2 * block, piece)
    to_tokens = []
    for i in b_peers[0]:
        to_tokens.append(send(send3.at[lax.rem(b + i, side)], recv3.at[b], s3.at[i], r3.at[i], b_dev(i, 0)))
    recv3[b] = send3[b]
    arrange(1)
    swap.wait_recv()
    swap_sib = send(other.at[c], other.at[c], s6.at[1], r6.at[1], sib_dev)

    for copy in to_tokens:
        copy.wait_recv()
    both = dot(cmat[...], recv3[...].reshape(size, piece))
    part_mixed = both[:lanes] + both[lanes : 2 * lanes]
    part_grad = both[2 * lanes :]
    for i in range(side):
        at = slice(i * toks, (i + 1) * toks)
        send4[i] = jnp.concatenate([part_mixed[at], part_grad[at]], axis=0).astype(BF16)
    home = []
    for i in range(1, side):
        home.append(send(send4.at[lax.rem(a + i, side)], recv4.at[a], s4.at[i], r4.at[i], a_dev(i)))
    recv4[a] = send4[a]

    swap_sib.wait_recv()
    hidden, gate_grad, up_grad = (
        jnp.concatenate([gathered(act.at[1], q), gathered(other, q)], axis=0) for q in range(3)
    )
    stores = []
    for k, (ref, out, left, right) in enumerate(
        ((gg_ref, gg_out, x_ref[...], gate_grad), (gu_ref, gu_out, x_ref[...], up_grad), (gd_ref, gd_out, hidden, do_ref[...]))
    ):
        ref[...] = dot_rows(left, right).astype(BF16)
        stores.append(pltpu.make_async_copy(ref, out.at[0], out_sem.at[k]))
        stores[-1].start()

    for copy in home:
        copy.wait_recv()
    final = recv4[0].astype(F32)
    for i in range(1, side):
        final = final + recv4[i].astype(F32)
    mixed_ref[...] = final[:toks].astype(BF16)
    grad_ref[...] = final[toks:].astype(BF16)
    for k, (ref, out) in enumerate(((mixed_ref, mixed_out), (grad_ref, grad_out))):
        stores.append(pltpu.make_async_copy(ref, out, out_sem.at[3 + k]))
        stores[-1].start()
    for copy in stores:
        copy.wait()
    for copy in started:
        copy.wait_send()


def store(*refs):
    ins, outs, held, sems = refs[:5], refs[5:10], refs[10:15], refs[15]
    loads = [pltpu.make_async_copy(ins[i], held[i], sems.at[0, i]) for i in range(5)]
    stores = [pltpu.make_async_copy(held[i], outs[i], sems.at[1, i]) for i in range(5)]
    for load in loads:
        load.start()
    for load, copy in zip(loads, stores):
        load.wait()
        copy.start()
    for copy in stores:
        copy.wait()


def on_device(side, tokens, cotangent, routes, gates, w_gate, w_up, w_down):
    toks, piece = tokens.shape
    top = routes.shape[1]
    width = w_gate.shape[2] // 2
    lanes = side * toks
    block = side * CAP
    rows = side * block
    part = rows // 4
    hbm = pl.BlockSpec(memory_space=pltpu.MemorySpace.HBM)
    dma = pltpu.SemaphoreType.DMA
    halves = (2, 2, 3 * part, width // CHIPS)
    pieces = (2, 2, CHIPS, 3 * part, width // CHIPS)
    results = pl.pallas_call(
        functools.partial(kernel, side),
        out_shape=(
            jax.ShapeDtypeStruct((toks, piece), BF16),
            jax.ShapeDtypeStruct((toks, piece), BF16),
            jax.ShapeDtypeStruct((1, piece, width), BF16),
            jax.ShapeDtypeStruct((1, piece, width), BF16),
            jax.ShapeDtypeStruct((1, width, piece), BF16),
        ),
        in_specs=[hbm] * 7,
        out_specs=(hbm,) * 5,
        scratch_shapes=[
            pltpu.VMEM((top, toks), jnp.int32),
            pltpu.VMEM((top, toks), F32),
            pltpu.VMEM((toks, piece), BF16),
            pltpu.VMEM((toks, piece), BF16),
            pltpu.VMEM((piece, width), BF16),
            pltpu.VMEM((piece, width), BF16),
            pltpu.VMEM((width, piece), BF16),
            dma((4,)), dma((5,)),
            pltpu.VMEM((2, piece, width), BF16),
            pltpu.VMEM((2, piece, width), BF16),
            pltpu.VMEM((2, width, piece), BF16),
            pltpu.VMEM((side, 2 * toks, piece), BF16),
            pltpu.VMEM((side, 2 * top, lanes), F32),
            pltpu.VMEM((3 * lanes, 2 * rows), BF16),
            pltpu.VMEM((2 * rows, 2 * rows), BF16),
            pltpu.VMEM((2 * rows, 2 * rows), BF16),
            pltpu.VMEM((side, 2 * block, piece), BF16),
            pltpu.VMEM((2, side, 2 * block, piece), BF16),
            pltpu.VMEM((2 * rows, piece), BF16),
            pltpu.VMEM((2 * rows, piece), BF16),
            pltpu.VMEM(pieces, BF16),
            pltpu.VMEM(pieces, BF16),
            pltpu.VMEM(pieces, F32),
            pltpu.VMEM(halves, BF16),
            pltpu.VMEM(halves, BF16),
            pltpu.VMEM(halves, BF16),
            pltpu.VMEM(halves, BF16),
            pltpu.VMEM(halves, BF16),
            pltpu.VMEM(halves, BF16),
            pltpu.VMEM((2, 2, CHIPS, 2, 3 * part, width // CHIPS), BF16),
            pltpu.VMEM((side, 2 * block, piece), BF16),
            pltpu.VMEM((side, 2 * block, piece), BF16),
            pltpu.VMEM((side, 2 * toks, piece), BF16),
            pltpu.VMEM((side, 2 * toks, piece), BF16),
            pltpu.VMEM((2, rows, piece), F32),
            pltpu.VMEM((2, CHIPS, 2, 3 * part, width // CHIPS), BF16),
            dma((2, 3)),
            dma((side,)), dma((side,)), dma((side,)), dma((side,)),
            dma((2, side)), dma((2, side)),
            dma((2,)), dma((2,)),
            dma((2, 6)), dma((2, 6)),
            dma((2, 14)), dma((2, 14)),
            dma((side,)), dma((side,)),
            dma((side,)), dma((side,)),
            dma((2,)), dma((2,)),
        ],
        compiler_params=pltpu.CompilerParams(
            collective_id=0, has_side_effects=True, vmem_limit_bytes=VMEM_LIMIT
        ),
        cost_estimate=pl.CostEstimate(
            flops=32 * rows * piece * width, bytes_accessed=6 * piece * width * 2, transcendentals=0
        ),
    )(tokens, cotangent, routes.T, gates.T, w_gate, w_up, w_down)
    return pl.pallas_call(
        store,
        out_shape=[jax.ShapeDtypeStruct(value.shape, value.dtype) for value in results],
        in_specs=[hbm] * 5,
        out_specs=[hbm] * 5,
        scratch_shapes=[pltpu.VMEM(value.shape, value.dtype) for value in results] + [dma((2, 5))],
        compiler_params=pltpu.CompilerParams(vmem_limit_bytes=VMEM_LIMIT),
    )(*results)


def solution(mesh):
    experts = mesh.shape["expert"]
    side = next(s for s in range(1, experts + 1) if s * s == experts)
    in_specs = (
        P(("expert", "dp"), "pipe"),
        P(("expert", "dp"), "pipe"),
        P(("expert", "dp"), None),
        P(("expert", "dp"), None),
        P("expert", "pipe", None),
        P("expert", "pipe", None),
        P("expert", None, "pipe"),
    )
    out_specs = (
        P(("expert", "dp"), "pipe"),
        P(("expert", "dp"), "pipe"),
        P("expert", "pipe", "dp"),
        P("expert", "pipe", "dp"),
        P("expert", "dp", "pipe"),
    )
    return jax.shard_map(
        functools.partial(on_device, side), mesh=mesh, in_specs=in_specs, out_specs=out_specs, check_vma=False
    )
```

```python
import functools

import jax
import jax.numpy as jnp
from jax import lax
from jax.experimental import pallas as pl
from jax.experimental.pallas import tpu as pltpu
from jax.sharding import PartitionSpec as P

CAP = 3
CHIPS = 4
VMEM_LIMIT = 60 * 1024 * 1024
MESH = pl.DeviceIdType.MESH
BF16, F32 = jnp.bfloat16, jnp.float32


def dot(left, right):
    return lax.dot_general(left, right, (((1,), (0,)), ((), ())), preferred_element_type=F32)


def dot_rows(left, right):
    return lax.dot_general(left, right, (((0,), (0,)), ((), ())), preferred_element_type=F32)


def dot_cols(left, right):
    return lax.dot_general(left, right, (((1,), (1,)), ((), ())), preferred_element_type=F32)


def silu_parts(value):
    sig = 1.0 / (1.0 + jnp.exp(-value))
    return value * sig, sig * (1.0 + value * (1.0 - sig))


def iota(shape, dim):
    return lax.broadcasted_iota(jnp.int32, shape, dim)


def kernel(
    side, tok_ref, cot_ref, routes_ref, gates_ref, wg_hbm, wu_hbm, wd_hbm,
    recv4, gg_out, gu_out, gd_out,
    routes_vmem, gates_vmem, gg_ref, gu_ref, gd_ref, in_sem, out_sem, wg, wu, wd,
    tokbuf, metabuf, cmat, perm, perm_back, send2, recv2, x_ref, do_ref, pair_send, pair_recv, mine,
    far_send, far_recv, imm_send, imm_recv, sum_send, sum_recv, act, send3, recv3, send4, acc, other,
    w_sem, s1, r1, s1m, r1m, s2, r2, sp, rp, sy, ry, s5, r5, s3, r3, s4, r4, s6, r6, s7, r7,
):
    toks, piece = tok_ref.shape
    top = routes_ref.shape[0]
    lanes = side * toks
    block = side * CAP
    rows = side * block
    size = 2 * rows
    width = wg.shape[2]
    cols = width // CHIPS
    part = rows // 4

    p, e, d = lax.axis_index("pipe"), lax.axis_index("expert"), lax.axis_index("dp")
    c, j = lax.rem(p, 2), lax.div(p, 2)
    hi, lo = lax.div(e, side), lax.rem(e, side)
    a, b = hi * (1 - c) + lo * c, lo * (1 - c) + hi * c
    sa, sb = side * (1 - c) + c, (1 - c) + side * c
    up, dn, far = lax.rem(j + 1, CHIPS), lax.rem(j + CHIPS - 1, CHIPS), lax.rem(j + 2, CHIPS)
    sib_dev = (2 * j + 1 - c, e, d)
    up_dev = (2 * up + c, e, d)
    dn_dev = (2 * dn + c, e, d)

    def a_dev(i):
        return (p, lax.rem(a + i, side) * sa + b * sb, d)

    def b_dev(i):
        return (p, a * sa + lax.rem(b + i, side) * sb, d)

    group_dev = (p, e, 1 - d)

    barrier = pltpu.get_barrier_semaphore()
    peers = [a_dev(i) for i in range(1, side)] + [b_dev(i) for i in range(1, side)]
    peers += [sib_dev, up_dev, dn_dev, group_dev]
    for dev in peers:
        pl.semaphore_signal(barrier, inc=1, device_id=dev, device_id_type=MESH)

    inputs = [
        pltpu.make_async_copy(routes_ref, routes_vmem, in_sem.at[0]),
        pltpu.make_async_copy(gates_ref, gates_vmem, in_sem.at[1]),
        pltpu.make_async_copy(tok_ref, tokbuf.at[a, pl.ds(0, toks)], in_sem.at[2]),
        pltpu.make_async_copy(cot_ref, tokbuf.at[a, pl.ds(toks, toks)], in_sem.at[3]),
    ]
    for load in inputs:
        load.start()
    loads = []
    for s in range(2):
        off = pl.multiple_of((d * s + (1 - d) * (1 - s)) * width, width)
        for k, (src, dst) in enumerate(
            (
                (wg_hbm.at[0, :, pl.ds(off, width)], wg.at[s]),
                (wu_hbm.at[0, :, pl.ds(off, width)], wu.at[s]),
                (wd_hbm.at[0, pl.ds(off, width), :], wd.at[s]),
            )
        ):
            loads.append(pltpu.make_async_copy(src, dst, w_sem.at[s, k]))
    for load in loads:
        load.start()

    started = []

    def send(src, dst, ssem, rsem, dev):
        copy = pltpu.make_async_remote_copy(
            src_ref=src, dst_ref=dst, send_sem=ssem, recv_sem=rsem, device_id=dev, device_id_type=MESH
        )
        copy.start()
        started.append(copy)
        return copy

    own = lax.div(iota((2 * top, lanes), 1), toks) == a
    for load in inputs:
        load.wait()
    values = jnp.concatenate([routes_vmem[...].astype(F32), gates_vmem[...]], axis=0)
    metabuf[a] = jnp.where(own, jnp.concatenate([values] * side, axis=1), 0.0)

    pl.semaphore_wait(barrier, len(peers))

    gather = []
    for i in range(1, side):
        gather.append(send(metabuf.at[a], metabuf.at[a], s1m.at[i], r1m.at[i], a_dev(i)))
    for i in range(1, side):
        gather.append(send(tokbuf.at[a], tokbuf.at[a], s1.at[i], r1.at[i], a_dev(i)))

    def sorted_place(at):
        at_b, at = lax.div(at, 2 * block), lax.rem(at, 2 * block)
        kind, at = lax.div(at, block), lax.rem(at, block)
        slot, at_a = lax.div(at, side), lax.rem(at, side)
        at_x, at_z = at_b * (1 - c) + at_a * c, at_a * (1 - c) + at_b * c
        return kind * rows + at_x * block + slot * side + at_z

    perm[...] = jnp.where(iota((size, size), 0) == sorted_place(iota((1, size), 1)), 1.0, 0.0).astype(BF16)
    perm_back[...] = jnp.where(iota((size, size), 1) == sorted_place(iota((size, 1), 0)), 1.0, 0.0).astype(BF16)
    first, second = iota((lanes, lanes), 0), iota((lanes, lanes), 1)
    earlier = (lax.div(first, toks) == lax.div(second, toks)) & (first < second)
    earlier = jnp.where(earlier, 1.0, 0.0).astype(BF16)
    slot, source = iota((block, lanes), 0), iota((block, lanes), 1)
    here = lax.rem(slot, side) == lax.div(source, toks)
    slot = lax.div(slot, side).astype(F32)

    for copy in gather[: side - 1]:
        copy.wait_recv()

    total = metabuf[0]
    for i in range(1, side):
        total = total + metabuf[i]
    routes, gates = total[:top], total[top:]
    named, weights = [], []
    for i in range(side):
        hit = routes == (a * sa + i * sb).astype(F32)
        named.append(jnp.sum(jnp.where(hit, 1.0, 0.0), axis=0, keepdims=True))
        weights.append(jnp.sum(jnp.where(hit, gates, 0.0), axis=0, keepdims=True))
    before = dot(jnp.concatenate(named, axis=0).astype(BF16), earlier)
    picks, scales = [], []
    for i in range(side):
        pick = jnp.where(here & (before[i : i + 1] == slot) & (named[i] > 0.5), 1.0, 0.0)
        picks.append(pick)
        scales.append(jnp.sum(pick * weights[i], axis=1, keepdims=True))
    place = jnp.concatenate(picks, axis=0).astype(BF16)
    scale = jnp.concatenate(scales, axis=0)

    for copy in gather[side - 1 :]:
        copy.wait_recv()
    xr = dot(place, tokbuf[:, 0:toks, :].reshape(lanes, piece))
    dr = dot(place, tokbuf[:, toks:, :].reshape(lanes, piece)) * scale
    for i in range(side):
        at = slice(block * i, block * (i + 1))
        send2[i] = jnp.concatenate([xr[at], dr[at]], axis=0).astype(BF16)
    to_experts = []
    for i in range(1, side):
        to_experts.append(send(send2.at[lax.rem(b + i, side)], recv2.at[b], s2.at[i], r2.at[i], b_dev(i)))
    recv2[b] = send2[b]

    empty = jnp.zeros((block, lanes), F32)
    wide = []
    for i in range(side):
        scaled = picks[i] * weights[i]
        high = scaled.astype(BF16).astype(F32)
        wide.append(jnp.concatenate([high, scaled - high, empty], axis=1))
        wide.append(jnp.concatenate([empty, empty, picks[i]], axis=1))
    cmat[...] = jnp.concatenate(wide, axis=0).T.astype(BF16)

    pair, fars, imms, sums, ups, dns, sibs, relays = ([None, None] for _ in range(8))
    ring = ((up, up_dev, dn, dn_dev), (dn, dn_dev, up, up_dev))

    def partials(s, core, out, cast):
        at = pl.ds(pl.multiple_of(core * 2 * part, 2 * part), 2 * part)
        xs, ds = x_ref[at, :], do_ref[at, :]
        for q, value in enumerate((dot(xs, wg[s]), dot(xs, wu[s]), dot_cols(ds, wd[s]))):
            for h in range(2):
                for k in range(CHIPS):
                    out[s, h, k, q * part : (q + 1) * part, :] = value[
                        h * part : (h + 1) * part, k * cols : (k + 1) * cols
                    ].astype(cast)

    def to_group(ref, k):
        quarter = rows // 2
        return send(
            ref.at[pl.ds(k % 2 * quarter, quarter)], ref.at[pl.ds(rows + k % 2 * quarter, quarter)],
            s7.at[k], r7.at[k], group_dev,
        )

    def project(s):
        partials(s, 1 - c, pair_send, BF16)
        pair[s] = send(pair_send.at[s], pair_recv.at[s], sp.at[s], rp.at[s], sib_dev)
        partials(s, c, mine, F32)

    def chip_sum(s, h, k):
        return mine[s, h, k] + pair_recv[s, h, k].astype(F32)

    def scatter_far(s):
        fars[s], imms[s] = [], []
        pair[s].wait_recv()
        for h in range(2):
            far_send[s, h] = chip_sum(s, h, far).astype(BF16)
            fars[s].append(send(far_send.at[s, h], far_recv.at[s, h], sy.at[s, h], ry.at[s, h], ring[h][1]))

    def scatter_near(s):
        for h in range(2):
            imm_send[s, h] = chip_sum(s, h, ring[h][2]).astype(BF16)
            imms[s].append(
                send(imm_send.at[s, h], imm_recv.at[s, h], sy.at[s, 2 + h], ry.at[s, 2 + h], ring[h][3])
            )

    def scatter_end(s):
        sums[s] = []
        for h in range(2):
            fars[s][h].wait_recv()
            sum_send[s, h] = (chip_sum(s, h, ring[h][0]) + far_recv[s, h].astype(F32)).astype(BF16)
            sums[s].append(
                send(sum_send.at[s, h], sum_recv.at[s, h], sy.at[s, 4 + h], ry.at[s, 4 + h], ring[h][1])
            )

    def pass_on(s, k, core, h, sem, dev):
        ref = act.at[s, core, k, h]
        return send(ref, ref, s5.at[s, sem], r5.at[s, sem], dev)

    def activate(s):
        ups[s], dns[s], sibs[s] = [], [], []
        for h in range(2):
            imms[s][h].wait_recv()
            sums[s][h].wait_recv()
            pre = chip_sum(s, h, j) + imm_recv[s, h].astype(F32) + sum_recv[s, h].astype(F32)
            gate, upv, hid_grad = pre[:part], pre[part : 2 * part], pre[2 * part :]
            silu, slope = silu_parts(gate)
            act[s, c, j, h, 0:part, :] = (silu * upv).astype(BF16)
            act[s, c, j, h, part : 2 * part, :] = (hid_grad * upv * slope).astype(BF16)
            act[s, c, j, h, 2 * part :, :] = (hid_grad * silu).astype(BF16)
            ups[s].append(pass_on(s, j, c, h, h, up_dev))
            dns[s].append(pass_on(s, j, c, h, 2 + h, dn_dev))
            sibs[s].append(pass_on(s, j, c, h, 6 + h, sib_dev))

    def relay(s):
        ups[s][0].wait_recv()
        relays[s] = [pass_on(s, dn, c, 0, 4, up_dev)]
        dns[s][1].wait_recv()
        relays[s].append(pass_on(s, up, c, 1, 5, dn_dev))
        sibs[s].append(pass_on(s, dn, c, 0, 8, sib_dev))
        sibs[s].append(pass_on(s, up, c, 1, 9, sib_dev))
        ups[s][1].wait_recv()
        sibs[s].append(pass_on(s, dn, c, 1, 10, sib_dev))
        dns[s][0].wait_recv()
        sibs[s].append(pass_on(s, up, c, 0, 11, sib_dev))

    def relay_end(s):
        for h in range(2):
            relays[s][h].wait_recv()
            sibs[s].append(pass_on(s, far, c, h, 12 + h, sib_dev))
        for copy in sibs[s]:
            copy.wait_recv()

    def gathered(ref, q):
        at = slice(q * part, (q + 1) * part)
        return jnp.concatenate(
            [
                jnp.concatenate([ref[core, k, h, at, :] for k in range(CHIPS)], axis=1)
                for core in range(2)
                for h in range(2)
            ],
            axis=0,
        )

    def answer(s):
        outs = dot(gathered(act.at[s], 0), wd[s])
        row_grads = dot_cols(gathered(act.at[s], 1), wg[s]) + dot_cols(gathered(act.at[s], 2), wu[s])
        return outs, row_grads

    for copy in to_experts:
        copy.wait_recv()
    found = dot(perm[...], recv2[...].reshape(size, piece)).astype(BF16)
    x_ref[:rows, :] = found[:rows]
    do_ref[:rows, :] = found[rows:]
    crossing = [to_group(x_ref, 0)]
    for load in loads:
        load.wait()
    project(0)
    project(1)
    scatter_far(0)
    scatter_near(0)
    scatter_far(1)
    scatter_end(0)
    scatter_near(1)
    activate(0)
    scatter_end(1)
    relay(0)
    activate(1)
    relay_end(0)
    acc[0], acc[1] = answer(0)
    relay(1)
    swap = send(act.at[0, c], other.at[c], s6.at[0], r6.at[0], group_dev)
    crossing += [to_group(x_ref, 1), to_group(do_ref, 2), to_group(do_ref, 3)]
    relay_end(1)
    outs, row_grads = answer(1)
    stacked = jnp.concatenate([acc[0] + outs, acc[1] + row_grads], axis=0).astype(BF16)
    send3[...] = dot(perm_back[...], stacked).astype(BF16).reshape(side, 2 * block, piece)
    to_tokens = []
    for i in range(1, side):
        to_tokens.append(send(send3.at[lax.rem(b + i, side)], recv3.at[b], s3.at[i], r3.at[i], b_dev(i)))
    recv3[b] = send3[b]
    swap.wait_recv()
    swap_sib = send(other.at[c], other.at[c], s6.at[1], r6.at[1], sib_dev)

    for copy in to_tokens:
        copy.wait_recv()
    both = dot(cmat[...], recv3[...].reshape(size, piece))
    part_mixed = both[:lanes] + both[lanes : 2 * lanes]
    part_grad = both[2 * lanes :]
    for i in range(side):
        at = slice(i * toks, (i + 1) * toks)
        send4[i] = jnp.concatenate([part_mixed[at], part_grad[at]], axis=0).astype(BF16)
    home = []
    for i in range(1, side):
        home.append(send(send4.at[lax.rem(a + i, side)], recv4.at[a], s4.at[i], r4.at[i], a_dev(i)))
    keep = pltpu.make_async_copy(send4.at[a], recv4.at[a], out_sem.at[3])
    keep.start()

    swap_sib.wait_recv()
    for copy in crossing:
        copy.wait_recv()
    hidden, gate_grad, up_grad = (
        jnp.concatenate([gathered(act.at[1], q), gathered(other, q)], axis=0) for q in range(3)
    )
    stores = []
    for k, (ref, out, left, right) in enumerate(
        ((gg_ref, gg_out, x_ref[...], gate_grad), (gu_ref, gu_out, x_ref[...], up_grad), (gd_ref, gd_out, hidden, do_ref[...]))
    ):
        ref[...] = dot_rows(left, right).astype(BF16)
        stores.append(pltpu.make_async_copy(ref, out.at[0], out_sem.at[k]))
        stores[-1].start()

    for copy in home:
        copy.wait_recv()
    keep.wait()
    for copy in stores:
        copy.wait()
    for copy in started:
        copy.wait_send()


def store(toks, parts_hbm, *refs):
    ins, outs, parts, held, both, sems = refs[:3], refs[3:8], refs[8], refs[9:12], refs[12:14], refs[14]
    load_parts = pltpu.make_async_copy(parts_hbm, parts, sems.at[0, 3])
    load_parts.start()
    loads = [pltpu.make_async_copy(ins[i], held[i], sems.at[0, i]) for i in range(3)]
    stores = [pltpu.make_async_copy(held[i], outs[2 + i], sems.at[1, i]) for i in range(3)]
    for load in loads:
        load.start()
    load_parts.wait()
    final = parts[0].astype(F32)
    for i in range(1, parts.shape[0]):
        final = final + parts[i].astype(F32)
    for i in range(2):
        both[i][...] = final[i * toks : (i + 1) * toks].astype(BF16)
        stores.append(pltpu.make_async_copy(both[i], outs[i], sems.at[1, 3 + i]))
        stores[-1].start()
    for load, copy in zip(loads, stores):
        load.wait()
        copy.start()
    for copy in stores:
        copy.wait()


def on_device(side, tokens, cotangent, routes, gates, w_gate, w_up, w_down):
    toks, piece = tokens.shape
    top = routes.shape[1]
    width = w_gate.shape[2] // 2
    lanes = side * toks
    block = side * CAP
    rows = side * block
    part = rows // 4
    tokens_out = [jax.ShapeDtypeStruct((toks, piece), BF16)] * 2
    grads = [jax.ShapeDtypeStruct((1, piece, width), BF16)] * 2 + [jax.ShapeDtypeStruct((1, width, piece), BF16)]
    hbm = pl.BlockSpec(memory_space=pltpu.MemorySpace.HBM)
    dma = pltpu.SemaphoreType.DMA
    halves = (2, 2, 3 * part, width // CHIPS)
    pieces = (2, 2, CHIPS, 3 * part, width // CHIPS)
    results = pl.pallas_call(
        functools.partial(kernel, side),
        out_shape=(jax.ShapeDtypeStruct((side, 2 * toks, piece), BF16), *grads),
        in_specs=[hbm] * 7,
        out_specs=(hbm,) * 4,
        scratch_shapes=[
            pltpu.VMEM((top, toks), jnp.int32),
            pltpu.VMEM((top, toks), F32),
            pltpu.VMEM((piece, width), BF16),
            pltpu.VMEM((piece, width), BF16),
            pltpu.VMEM((width, piece), BF16),
            dma((4,)), dma((5,)),
            pltpu.VMEM((2, piece, width), BF16),
            pltpu.VMEM((2, piece, width), BF16),
            pltpu.VMEM((2, width, piece), BF16),
            pltpu.VMEM((side, 2 * toks, piece), BF16),
            pltpu.VMEM((side, 2 * top, lanes), F32),
            pltpu.VMEM((3 * lanes, 2 * rows), BF16),
            pltpu.VMEM((2 * rows, 2 * rows), BF16),
            pltpu.VMEM((2 * rows, 2 * rows), BF16),
            pltpu.VMEM((side, 2 * block, piece), BF16),
            pltpu.VMEM((side, 2 * block, piece), BF16),
            pltpu.VMEM((2 * rows, piece), BF16),
            pltpu.VMEM((2 * rows, piece), BF16),
            pltpu.VMEM(pieces, BF16),
            pltpu.VMEM(pieces, BF16),
            pltpu.VMEM(pieces, F32),
            pltpu.VMEM(halves, BF16),
            pltpu.VMEM(halves, BF16),
            pltpu.VMEM(halves, BF16),
            pltpu.VMEM(halves, BF16),
            pltpu.VMEM(halves, BF16),
            pltpu.VMEM(halves, BF16),
            pltpu.VMEM((2, 2, CHIPS, 2, 3 * part, width // CHIPS), BF16),
            pltpu.VMEM((side, 2 * block, piece), BF16),
            pltpu.VMEM((side, 2 * block, piece), BF16),
            pltpu.VMEM((side, 2 * toks, piece), BF16),
            pltpu.VMEM((2, rows, piece), F32),
            pltpu.VMEM((2, CHIPS, 2, 3 * part, width // CHIPS), BF16),
            dma((2, 3)),
            dma((side,)), dma((side,)), dma((side,)), dma((side,)),
            dma((side,)), dma((side,)),
            dma((2,)), dma((2,)),
            dma((2, 6)), dma((2, 6)),
            dma((2, 14)), dma((2, 14)),
            dma((side,)), dma((side,)),
            dma((side,)), dma((side,)),
            dma((2,)), dma((2,)),
            dma((4,)), dma((4,)),
        ],
        compiler_params=pltpu.CompilerParams(
            collective_id=0, has_side_effects=True, vmem_limit_bytes=VMEM_LIMIT
        ),
        cost_estimate=pl.CostEstimate(
            flops=32 * rows * piece * width, bytes_accessed=6 * piece * width * 2, transcendentals=0
        ),
    )(tokens, cotangent, routes.T, gates.T, w_gate, w_up, w_down)
    return pl.pallas_call(
        functools.partial(store, toks),
        out_shape=[*tokens_out, *grads],
        in_specs=[hbm] * 4,
        out_specs=[hbm] * 5,
        scratch_shapes=[pltpu.VMEM(value.shape, value.dtype) for value in (*results, *tokens_out)] + [dma((2, 5))],
        compiler_params=pltpu.CompilerParams(vmem_limit_bytes=VMEM_LIMIT),
    )(*results)


def solution(mesh):
    experts = mesh.shape["expert"]
    side = next(s for s in range(1, experts + 1) if s * s == experts)
    in_specs = (
        P(("expert", "dp"), "pipe"),
        P(("expert", "dp"), "pipe"),
        P(("expert", "dp"), None),
        P(("expert", "dp"), None),
        P("expert", "pipe", None),
        P("expert", "pipe", None),
        P("expert", None, "pipe"),
    )
    out_specs = (
        P(("expert", "dp"), "pipe"),
        P(("expert", "dp"), "pipe"),
        P("expert", "pipe", "dp"),
        P("expert", "pipe", "dp"),
        P("expert", "dp", "pipe"),
    )
    return jax.shard_map(
        functools.partial(on_device, side), mesh=mesh, in_specs=in_specs, out_specs=out_specs, check_vma=False
    )
```

```python
import functools

import jax
import jax.numpy as jnp
from jax import lax
from jax.experimental import pallas as pl
from jax.experimental.pallas import tpu as pltpu
from jax.sharding import PartitionSpec as P

CAP = 3
CHIPS = 4
VMEM_LIMIT = 60 * 1024 * 1024
MESH = pl.DeviceIdType.MESH
BF16, F32 = jnp.bfloat16, jnp.float32


def dot(left, right):
    return lax.dot_general(left, right, (((1,), (0,)), ((), ())), preferred_element_type=F32)


def dot_rows(left, right):
    return lax.dot_general(left, right, (((0,), (0,)), ((), ())), preferred_element_type=F32)


def dot_cols(left, right):
    return lax.dot_general(left, right, (((1,), (1,)), ((), ())), preferred_element_type=F32)


def silu_parts(value):
    sig = 1.0 / (1.0 + jnp.exp(-value))
    return value * sig, sig * (1.0 + value * (1.0 - sig))


def iota(shape, dim):
    return lax.broadcasted_iota(jnp.int32, shape, dim)


def kernel(
    side, tok_ref, cot_ref, routes_ref, gates_ref, wg_hbm, wu_hbm, wd_hbm,
    recv4, gg_out, gu_out, gd_out,
    routes_vmem, gates_vmem, gg_ref, gu_ref, gd_ref, in_sem, out_sem, wg, wu, wd,
    tokbuf, metabuf, cmat, perm, perm_back, send2, recv2, x_ref, do_ref, pair_send, pair_recv, mine,
    far_send, far_recv, imm_send, imm_recv, sum_send, sum_recv, act, send3, recv3, send4, acc, other,
    w_sem, s1, r1, s1m, r1m, s2, r2, sp, rp, sy, ry, s5, r5, s3, r3, s4, r4, s6, r6, s7, r7,
):
    toks, piece = tok_ref.shape
    top = routes_ref.shape[0]
    lanes = side * toks
    block = side * CAP
    rows = side * block
    size = 2 * rows
    width = wg.shape[2]
    cols = width // CHIPS
    part = rows // 4
    feat = piece // 2
    halves = [slice(f * feat, (f + 1) * feat) for f in range(2)]

    p, e, d = lax.axis_index("pipe"), lax.axis_index("expert"), lax.axis_index("dp")
    c, j = lax.rem(p, 2), lax.div(p, 2)
    hi, lo = lax.div(e, side), lax.rem(e, side)
    a, b = hi * (1 - c) + lo * c, lo * (1 - c) + hi * c
    sa, sb = side * (1 - c) + c, (1 - c) + side * c
    up, dn, far = lax.rem(j + 1, CHIPS), lax.rem(j + CHIPS - 1, CHIPS), lax.rem(j + 2, CHIPS)
    sib_dev = (2 * j + 1 - c, e, d)
    up_dev = (2 * up + c, e, d)
    dn_dev = (2 * dn + c, e, d)

    def a_dev(i):
        return (p, lax.rem(a + i, side) * sa + b * sb, d)

    def b_dev(i):
        return (p, a * sa + lax.rem(b + i, side) * sb, d)

    group_dev = (p, e, 1 - d)

    barrier = pltpu.get_barrier_semaphore()
    peers = [a_dev(i) for i in range(1, side)] + [b_dev(i) for i in range(1, side)]
    peers += [sib_dev, up_dev, dn_dev, group_dev]
    for dev in peers:
        pl.semaphore_signal(barrier, inc=1, device_id=dev, device_id_type=MESH)

    inputs = [
        pltpu.make_async_copy(routes_ref, routes_vmem, in_sem.at[0]),
        pltpu.make_async_copy(gates_ref, gates_vmem, in_sem.at[1]),
    ]
    for f in range(2):
        for k, ref in enumerate((tok_ref, cot_ref)):
            inputs.append(
                pltpu.make_async_copy(
                    ref.at[:, pl.ds(f * feat, feat)], tokbuf.at[f, a, pl.ds(k * toks, toks)], in_sem.at[2 + 2 * f + k]
                )
            )
    for load in inputs:
        load.start()
    loads = []
    for s in range(2):
        off = pl.multiple_of((d * s + (1 - d) * (1 - s)) * width, width)
        for k, (src, dst) in enumerate(
            (
                (wg_hbm.at[0, :, pl.ds(off, width)], wg.at[s]),
                (wu_hbm.at[0, :, pl.ds(off, width)], wu.at[s]),
                (wd_hbm.at[0, pl.ds(off, width), :], wd.at[s]),
            )
        ):
            loads.append(pltpu.make_async_copy(src, dst, w_sem.at[s, k]))
    for load in loads:
        load.start()

    started = []

    def send(src, dst, ssem, rsem, dev):
        copy = pltpu.make_async_remote_copy(
            src_ref=src, dst_ref=dst, send_sem=ssem, recv_sem=rsem, device_id=dev, device_id_type=MESH
        )
        copy.start()
        started.append(copy)
        return copy

    own = lax.div(iota((2 * top, lanes), 1), toks) == a
    for load in inputs:
        load.wait()
    values = jnp.concatenate([routes_vmem[...].astype(F32), gates_vmem[...]], axis=0)
    metabuf[a] = jnp.where(own, jnp.concatenate([values] * side, axis=1), 0.0)

    pl.semaphore_wait(barrier, len(peers))

    gather = []
    for i in range(1, side):
        gather.append(send(metabuf.at[a], metabuf.at[a], s1m.at[i], r1m.at[i], a_dev(i)))
    for f in range(2):
        for i in range(1, side):
            gather.append(send(tokbuf.at[f, a], tokbuf.at[f, a], s1.at[f, i], r1.at[f, i], a_dev(i)))

    def sorted_place(at):
        at_b, at = lax.div(at, 2 * block), lax.rem(at, 2 * block)
        kind, at = lax.div(at, block), lax.rem(at, block)
        slot, at_a = lax.div(at, side), lax.rem(at, side)
        at_x, at_z = at_b * (1 - c) + at_a * c, at_a * (1 - c) + at_b * c
        return kind * rows + at_x * block + slot * side + at_z

    perm[...] = jnp.where(iota((size, size), 0) == sorted_place(iota((1, size), 1)), 1.0, 0.0).astype(BF16)
    perm_back[...] = jnp.where(iota((size, size), 1) == sorted_place(iota((size, 1), 0)), 1.0, 0.0).astype(BF16)
    first, second = iota((lanes, lanes), 0), iota((lanes, lanes), 1)
    earlier = (lax.div(first, toks) == lax.div(second, toks)) & (first < second)
    earlier = jnp.where(earlier, 1.0, 0.0).astype(BF16)
    slot, source = iota((block, lanes), 0), iota((block, lanes), 1)
    here = lax.rem(slot, side) == lax.div(source, toks)
    slot = lax.div(slot, side).astype(F32)

    for copy in gather[: side - 1]:
        copy.wait_recv()

    total = metabuf[0]
    for i in range(1, side):
        total = total + metabuf[i]
    routes, gates = total[:top], total[top:]
    named, weights = [], []
    for i in range(side):
        hit = routes == (a * sa + i * sb).astype(F32)
        named.append(jnp.sum(jnp.where(hit, 1.0, 0.0), axis=0, keepdims=True))
        weights.append(jnp.sum(jnp.where(hit, gates, 0.0), axis=0, keepdims=True))
    before = dot(jnp.concatenate(named, axis=0).astype(BF16), earlier)
    picks, scales = [], []
    for i in range(side):
        pick = jnp.where(here & (before[i : i + 1] == slot) & (named[i] > 0.5), 1.0, 0.0)
        picks.append(pick)
        scales.append(jnp.sum(pick * weights[i], axis=1, keepdims=True))
    place = jnp.concatenate(picks, axis=0).astype(BF16)
    scale = jnp.concatenate(scales, axis=0)

    to_experts = []
    for f in range(2):
        for copy in gather[(f + 1) * (side - 1) : (f + 2) * (side - 1)]:
            copy.wait_recv()
        xr = dot(place, tokbuf[f, :, 0:toks, :].reshape(lanes, feat))
        dr = dot(place, tokbuf[f, :, toks:, :].reshape(lanes, feat)) * scale
        for i in range(side):
            at = slice(block * i, block * (i + 1))
            send2[f, i] = jnp.concatenate([xr[at], dr[at]], axis=0).astype(BF16)
        for i in range(1, side):
            to_experts.append(
                send(send2.at[f, lax.rem(b + i, side)], recv2.at[f, b], s2.at[f, i], r2.at[f, i], b_dev(i))
            )
        recv2[f, b] = send2[f, b]

    empty = jnp.zeros((block, lanes), F32)
    wide = []
    for i in range(side):
        scaled = picks[i] * weights[i]
        high = scaled.astype(BF16).astype(F32)
        wide.append(jnp.concatenate([high, scaled - high, empty], axis=1))
        wide.append(jnp.concatenate([empty, empty, picks[i]], axis=1))
    cmat[...] = jnp.concatenate(wide, axis=0).T.astype(BF16)

    pair, fars, imms, sums, ups, dns, sibs, relays = ([None, None] for _ in range(8))
    ring = ((up, up_dev, dn, dn_dev), (dn, dn_dev, up, up_dev))

    def partials(s, core, out, cast):
        at = pl.ds(pl.multiple_of(core * 2 * part, 2 * part), 2 * part)
        xs, ds = x_ref[at, :], do_ref[at, :]
        for q, value in enumerate((dot(xs, wg[s]), dot(xs, wu[s]), dot_cols(ds, wd[s]))):
            for h in range(2):
                for k in range(CHIPS):
                    out[s, h, k, q * part : (q + 1) * part, :] = value[
                        h * part : (h + 1) * part, k * cols : (k + 1) * cols
                    ].astype(cast)

    def to_group(ref, k):
        quarter = rows // 2
        return send(
            ref.at[pl.ds(k % 2 * quarter, quarter)], ref.at[pl.ds(rows + k % 2 * quarter, quarter)],
            s7.at[k], r7.at[k], group_dev,
        )

    def project(s):
        partials(s, 1 - c, pair_send, BF16)
        pair[s] = send(pair_send.at[s], pair_recv.at[s], sp.at[s], rp.at[s], sib_dev)
        partials(s, c, mine, F32)

    def chip_sum(s, h, k):
        return mine[s, h, k] + pair_recv[s, h, k].astype(F32)

    def scatter_far(s):
        fars[s], imms[s] = [], []
        pair[s].wait_recv()
        for h in range(2):
            far_send[s, h] = chip_sum(s, h, far).astype(BF16)
            fars[s].append(send(far_send.at[s, h], far_recv.at[s, h], sy.at[s, h], ry.at[s, h], ring[h][1]))

    def scatter_near(s):
        for h in range(2):
            imm_send[s, h] = chip_sum(s, h, ring[h][2]).astype(BF16)
            imms[s].append(
                send(imm_send.at[s, h], imm_recv.at[s, h], sy.at[s, 2 + h], ry.at[s, 2 + h], ring[h][3])
            )

    def scatter_end(s):
        sums[s] = []
        for h in range(2):
            fars[s][h].wait_recv()
            sum_send[s, h] = (chip_sum(s, h, ring[h][0]) + far_recv[s, h].astype(F32)).astype(BF16)
            sums[s].append(
                send(sum_send.at[s, h], sum_recv.at[s, h], sy.at[s, 4 + h], ry.at[s, 4 + h], ring[h][1])
            )

    def pass_on(s, k, core, h, sem, dev):
        ref = act.at[s, core, k, h]
        return send(ref, ref, s5.at[s, sem], r5.at[s, sem], dev)

    def activate(s):
        ups[s], dns[s], sibs[s] = [], [], []
        for h in range(2):
            imms[s][h].wait_recv()
            sums[s][h].wait_recv()
            pre = chip_sum(s, h, j) + imm_recv[s, h].astype(F32) + sum_recv[s, h].astype(F32)
            gate, upv, hid_grad = pre[:part], pre[part : 2 * part], pre[2 * part :]
            silu, slope = silu_parts(gate)
            act[s, c, j, h, 0:part, :] = (silu * upv).astype(BF16)
            act[s, c, j, h, part : 2 * part, :] = (hid_grad * upv * slope).astype(BF16)
            act[s, c, j, h, 2 * part :, :] = (hid_grad * silu).astype(BF16)
            ups[s].append(pass_on(s, j, c, h, h, up_dev))
            dns[s].append(pass_on(s, j, c, h, 2 + h, dn_dev))
            sibs[s].append(pass_on(s, j, c, h, 6 + h, sib_dev))

    def relay(s):
        ups[s][0].wait_recv()
        relays[s] = [pass_on(s, dn, c, 0, 4, up_dev)]
        dns[s][1].wait_recv()
        relays[s].append(pass_on(s, up, c, 1, 5, dn_dev))
        sibs[s].append(pass_on(s, dn, c, 0, 8, sib_dev))
        sibs[s].append(pass_on(s, up, c, 1, 9, sib_dev))
        ups[s][1].wait_recv()
        sibs[s].append(pass_on(s, dn, c, 1, 10, sib_dev))
        dns[s][0].wait_recv()
        sibs[s].append(pass_on(s, up, c, 0, 11, sib_dev))

    def relay_end(s):
        for h in range(2):
            relays[s][h].wait_recv()
            sibs[s].append(pass_on(s, far, c, h, 12 + h, sib_dev))
        for copy in sibs[s]:
            copy.wait_recv()

    def gathered(ref, q):
        at = slice(q * part, (q + 1) * part)
        return jnp.concatenate(
            [
                jnp.concatenate([ref[core, k, h, at, :] for k in range(CHIPS)], axis=1)
                for core in range(2)
                for h in range(2)
            ],
            axis=0,
        )

    for copy in to_experts:
        copy.wait_recv()
    for f, at in enumerate(halves):
        found = dot(perm[...], recv2[f].reshape(size, feat)).astype(BF16)
        x_ref[:rows, at] = found[:rows]
        do_ref[:rows, at] = found[rows:]
    crossing = [to_group(x_ref, 0)]
    for load in loads:
        load.wait()
    project(0)
    project(1)
    scatter_far(0)
    scatter_near(0)
    scatter_far(1)
    scatter_end(0)
    scatter_near(1)
    activate(0)
    scatter_end(1)
    relay(0)
    activate(1)
    relay_end(0)
    acc[0] = dot(gathered(act.at[0], 0), wd[0])
    acc[1] = dot_cols(gathered(act.at[0], 1), wg[0]) + dot_cols(gathered(act.at[0], 2), wu[0])
    relay(1)
    swap = send(act.at[0, c], other.at[c], s6.at[0], r6.at[0], group_dev)
    crossing += [to_group(x_ref, 1), to_group(do_ref, 2), to_group(do_ref, 3)]
    relay_end(1)
    hidden, gate_grad, up_grad = (gathered(act.at[1], q) for q in range(3))
    to_tokens = []
    for f, at in enumerate(halves):
        outs = acc[0, :, at] + dot(hidden, wd[1, :, at])
        row_grads = acc[1, :, at] + dot_cols(gate_grad, wg[1, at, :]) + dot_cols(up_grad, wu[1, at, :])
        stacked = jnp.concatenate([outs, row_grads], axis=0).astype(BF16)
        send3[f] = dot(perm_back[...], stacked).astype(BF16).reshape(side, 2 * block, feat)
        for i in range(1, side):
            to_tokens.append(
                send(send3.at[f, lax.rem(b + i, side)], recv3.at[f, b], s3.at[f, i], r3.at[f, i], b_dev(i))
            )
        recv3[f, b] = send3[f, b]
    swap.wait_recv()
    swap_sib = send(other.at[c], other.at[c], s6.at[1], r6.at[1], sib_dev)

    home = []
    for f in range(2):
        for copy in to_tokens[f * (side - 1) : (f + 1) * (side - 1)]:
            copy.wait_recv()
        both = dot(cmat[...], recv3[f].reshape(size, feat))
        part_mixed = both[:lanes] + both[lanes : 2 * lanes]
        part_grad = both[2 * lanes :]
        for i in range(side):
            at = slice(i * toks, (i + 1) * toks)
            send4[f, i] = jnp.concatenate([part_mixed[at], part_grad[at]], axis=0).astype(BF16)
        for i in range(1, side):
            home.append(
                send(send4.at[f, lax.rem(a + i, side)], recv4.at[f, a], s4.at[f, i], r4.at[f, i], a_dev(i))
            )
        home.append(pltpu.make_async_copy(send4.at[f, a], recv4.at[f, a], out_sem.at[3 + f]))
        home[-1].start()

    swap_sib.wait_recv()
    for copy in crossing:
        copy.wait_recv()
    hidden, gate_grad, up_grad = (
        jnp.concatenate([mine_q, gathered(other, q)], axis=0)
        for q, mine_q in enumerate((hidden, gate_grad, up_grad))
    )
    stores = []
    for k, (ref, out, left, right) in enumerate(
        ((gg_ref, gg_out, x_ref[...], gate_grad), (gu_ref, gu_out, x_ref[...], up_grad), (gd_ref, gd_out, hidden, do_ref[...]))
    ):
        ref[...] = dot_rows(left, right).astype(BF16)
        stores.append(pltpu.make_async_copy(ref, out.at[0], out_sem.at[k]))
        stores[-1].start()

    for copy in home[side - 1 :: side]:
        copy.wait()
    for f in range(2):
        for copy in home[f * side : f * side + side - 1]:
            copy.wait_recv()
    for copy in stores:
        copy.wait()
    for copy in started:
        copy.wait_send()


def store(toks, parts_hbm, *refs):
    ins, outs, parts, held, both, sems = refs[:3], refs[3:8], refs[8], refs[9:12], refs[12:14], refs[14]
    load_parts = pltpu.make_async_copy(parts_hbm, parts, sems.at[0, 3])
    load_parts.start()
    loads = [pltpu.make_async_copy(ins[i], held[i], sems.at[0, i]) for i in range(3)]
    stores = [pltpu.make_async_copy(held[i], outs[2 + i], sems.at[1, i]) for i in range(3)]
    for load in loads:
        load.start()
    load_parts.wait()
    final = parts[:, 0].astype(F32)
    for i in range(1, parts.shape[1]):
        final = final + parts[:, i].astype(F32)
    final = jnp.concatenate([final[0], final[1]], axis=1)
    for i in range(2):
        both[i][...] = final[i * toks : (i + 1) * toks].astype(BF16)
        stores.append(pltpu.make_async_copy(both[i], outs[i], sems.at[1, 3 + i]))
        stores[-1].start()
    for load, copy in zip(loads, stores):
        load.wait()
        copy.start()
    for copy in stores:
        copy.wait()


def on_device(side, tokens, cotangent, routes, gates, w_gate, w_up, w_down):
    toks, piece = tokens.shape
    top = routes.shape[1]
    width = w_gate.shape[2] // 2
    lanes = side * toks
    block = side * CAP
    rows = side * block
    part = rows // 4
    tokens_out = [jax.ShapeDtypeStruct((toks, piece), BF16)] * 2
    grads = [jax.ShapeDtypeStruct((1, piece, width), BF16)] * 2 + [jax.ShapeDtypeStruct((1, width, piece), BF16)]
    hbm = pl.BlockSpec(memory_space=pltpu.MemorySpace.HBM)
    dma = pltpu.SemaphoreType.DMA
    feat = piece // 2
    halves = (2, 2, 3 * part, width // CHIPS)
    pieces = (2, 2, CHIPS, 3 * part, width // CHIPS)
    results = pl.pallas_call(
        functools.partial(kernel, side),
        out_shape=(jax.ShapeDtypeStruct((2, side, 2 * toks, feat), BF16), *grads),
        in_specs=[hbm] * 7,
        out_specs=(hbm,) * 4,
        scratch_shapes=[
            pltpu.VMEM((top, toks), jnp.int32),
            pltpu.VMEM((top, toks), F32),
            pltpu.VMEM((piece, width), BF16),
            pltpu.VMEM((piece, width), BF16),
            pltpu.VMEM((width, piece), BF16),
            dma((6,)), dma((5,)),
            pltpu.VMEM((2, piece, width), BF16),
            pltpu.VMEM((2, piece, width), BF16),
            pltpu.VMEM((2, width, piece), BF16),
            pltpu.VMEM((2, side, 2 * toks, feat), BF16),
            pltpu.VMEM((side, 2 * top, lanes), F32),
            pltpu.VMEM((3 * lanes, 2 * rows), BF16),
            pltpu.VMEM((2 * rows, 2 * rows), BF16),
            pltpu.VMEM((2 * rows, 2 * rows), BF16),
            pltpu.VMEM((2, side, 2 * block, feat), BF16),
            pltpu.VMEM((2, side, 2 * block, feat), BF16),
            pltpu.VMEM((2 * rows, piece), BF16),
            pltpu.VMEM((2 * rows, piece), BF16),
            pltpu.VMEM(pieces, BF16),
            pltpu.VMEM(pieces, BF16),
            pltpu.VMEM(pieces, F32),
            pltpu.VMEM(halves, BF16),
            pltpu.VMEM(halves, BF16),
            pltpu.VMEM(halves, BF16),
            pltpu.VMEM(halves, BF16),
            pltpu.VMEM(halves, BF16),
            pltpu.VMEM(halves, BF16),
            pltpu.VMEM((2, 2, CHIPS, 2, 3 * part, width // CHIPS), BF16),
            pltpu.VMEM((2, side, 2 * block, feat), BF16),
            pltpu.VMEM((2, side, 2 * block, feat), BF16),
            pltpu.VMEM((2, side, 2 * toks, feat), BF16),
            pltpu.VMEM((2, rows, piece), F32),
            pltpu.VMEM((2, CHIPS, 2, 3 * part, width // CHIPS), BF16),
            dma((2, 3)),
            dma((2, side)), dma((2, side)), dma((side,)), dma((side,)),
            dma((2, side)), dma((2, side)),
            dma((2,)), dma((2,)),
            dma((2, 6)), dma((2, 6)),
            dma((2, 14)), dma((2, 14)),
            dma((2, side)), dma((2, side)),
            dma((2, side)), dma((2, side)),
            dma((2,)), dma((2,)),
            dma((4,)), dma((4,)),
        ],
        compiler_params=pltpu.CompilerParams(
            collective_id=0, has_side_effects=True, vmem_limit_bytes=VMEM_LIMIT
        ),
        cost_estimate=pl.CostEstimate(
            flops=32 * rows * piece * width, bytes_accessed=6 * piece * width * 2, transcendentals=0
        ),
    )(tokens, cotangent, routes.T, gates.T, w_gate, w_up, w_down)
    return pl.pallas_call(
        functools.partial(store, toks),
        out_shape=[*tokens_out, *grads],
        in_specs=[hbm] * 4,
        out_specs=[hbm] * 5,
        scratch_shapes=[pltpu.VMEM(value.shape, value.dtype) for value in (*results, *tokens_out)] + [dma((2, 5))],
        compiler_params=pltpu.CompilerParams(vmem_limit_bytes=VMEM_LIMIT),
    )(*results)


def solution(mesh):
    experts = mesh.shape["expert"]
    side = next(s for s in range(1, experts + 1) if s * s == experts)
    in_specs = (
        P(("expert", "dp"), "pipe"),
        P(("expert", "dp"), "pipe"),
        P(("expert", "dp"), None),
        P(("expert", "dp"), None),
        P("expert", "pipe", None),
        P("expert", "pipe", None),
        P("expert", None, "pipe"),
    )
    out_specs = (
        P(("expert", "dp"), "pipe"),
        P(("expert", "dp"), "pipe"),
        P("expert", "pipe", "dp"),
        P("expert", "pipe", "dp"),
        P("expert", "dp", "pipe"),
    )
    return jax.shard_map(
        functools.partial(on_device, side), mesh=mesh, in_specs=in_specs, out_specs=out_specs, check_vma=False
    )
```
